256 devices in a mesh: row: 8 (over x, core), col: 32 (over y, z).
Axes of the slice: x: 4, y: 4, z: 8, core: 2. Of those that a mesh axis runs over, the one named last changes fastest.
Arguments:
- features: bfloat16 [65536, 256], P(('row', 'col'))
- weight_self: bfloat16 [256, 256], replicated, may hold values from -0.375 to 0.375
- weight_neigh: bfloat16 [256, 256], replicated, may hold values from -0.375 to 0.375
- norm_gain: float32 [256], replicated, may hold values from 0.1 to 1.9
- norm_shift: float32 [256], replicated, may hold values from -3 to 3
- upstream: bfloat16 [65536, 256], P(('row', 'col')), may hold values from -6 to 6
- source_index: int32 [8, 32, 32, 256], P('row', 'col'), may hold values from 0 to 2047
- target_index: int32 [8, 32, 32, 256], P('row', 'col'), may hold values from 0 to 255
- edge_weight: bfloat16 [8, 32, 32, 256], P('row', 'col'), may hold values from 0.029907227 to 0.29882812
- edge_count: int32 [8, 32, 32], P('row', 'col'), may hold values from 0 to 256, as said below
Outputs:
- grad_x: bfloat16 [65536, 256], P(('row', 'col'))
- grad_w_self: float32 [256, 256], replicated
- grad_w_neigh: float32 [256, 256], replicated
- grad_gain: float32 [256], replicated
- grad_shift: float32 [256], replicated
The draws below stay inside these ranges and needn't reach their ends.
Inputs may be any that keep to these rules, and one draw needn't show every extreme that they name: `edge_count`: some tile and block have exactly 256 live slots; whole tiles may be empty.
All inputs are finite; a program needn't handle non-finite values.
Results may differ from the reference program's by a relative error of at most 0.0057.
Values may be sent and summed in bfloat16 or wider, within the bound.
No kernel may reach another device: no remote copies, remote signals or barrier semaphores. Data moves between devices by JAX's collectives and lax.ppermute only.
A program may use at most 64 MiB of HBM per device.

```python
import math
import jax
import jax.numpy as jnp
from jax import lax

FEAT = 256
NODE_DEV = 256
EDGE_CAP = 256
NODES = 65536
N_ROW = 8
N_COL = 32


def draw_edge_count(key, part):
    key = jax.random.fold_in(key, 11)
    keys = jax.random.split(key, 4)
    shape = (N_ROW, N_COL, N_COL)
    base = jax.random.randint(keys[0], shape, 0, EDGE_CAP // 2 + 1)
    heavy = jax.random.randint(keys[1], shape, 0, 4) == 0
    tile_live = jax.random.randint(keys[2], (N_ROW, N_COL, 1), 0, 16) > 0
    counts = jnp.where(heavy, EDGE_CAP, base) * tile_live.astype(jnp.int32)
    position = jax.random.randint(keys[3], (), 0, N_ROW * N_COL * N_COL)
    counts = counts.reshape(-1).at[position].set(EDGE_CAP).reshape(shape)
    return counts.astype(jnp.int32)


def draw_features(key, part):
    key = jax.random.fold_in(key, 12)
    keys = jax.random.split(key, 3)
    node_pos = jnp.arange(NODES, dtype=jnp.float32)[:, None]
    rising = 0.5 + node_pos / NODES
    row_scale = jnp.exp(jax.random.uniform(keys[1], (NODES, 1), jnp.float32, math.log(0.3), math.log(3.0)))
    col_scale = jnp.exp(jax.random.uniform(keys[2], (1, FEAT), jnp.float32, math.log(0.6), math.log(1.7)))
    values = jax.random.normal(keys[0], (NODES, FEAT), jnp.float32)
    return (values * row_scale * rising * col_scale).astype(jnp.bfloat16)


def draw_upstream(key, part):
    key = jax.random.fold_in(key, 13)
    keys = jax.random.split(key, 2)
    offset = 0.4 * jax.random.normal(keys[1], (1, FEAT), jnp.float32)
    values = jax.random.normal(keys[0], (NODES, FEAT), jnp.float32)
    return jnp.clip(values + offset, -6.0, 6.0).astype(jnp.bfloat16)


def touch_ends(result, own_key, least, largest):
    shape = result.shape
    place = [jax.random.randint(jax.random.fold_in(own_key, axis), (), 0, shape[axis]) for axis in range(len(shape))]
    result = result.at[tuple(place)].set(least)
    longest = shape.index(max(shape))
    place[longest] = (place[longest] + 1) % shape[longest]
    return result.at[tuple(place)].set(largest)


def block_levels(stream_key, extent, pieces, smallest, top_value):
    loudness, own = 1.0, jax.random.fold_in(stream_key, 6)
    for dim, blocks in pieces:
        steps = jnp.exp(jax.random.uniform(jax.random.fold_in(own, dim), (blocks,), jnp.float32, smallest / len(pieces), top_value / len(pieces)))
        loudness = loudness * jnp.repeat(steps, extent[dim] // blocks).reshape([-1 if axis == dim else 1 for axis in range(len(extent))])
    return loudness


def gaussian(key, extent, scale, reach, kind=jnp.bfloat16):
    values = scale * jax.random.normal(key, extent, jnp.float32)
    return jnp.clip(values, min=-reach, max=reach).astype(kind)


def setup_inputs(seed: int = 0) -> dict:
    key_list = jax.random.split(jax.random.key(seed), 11)
    return {
        "features": draw_features(jax.random.fold_in(key_list[10], 71), 0),
        "weight_self": gaussian(key_list[1], (FEAT, FEAT), FEAT ** -0.5, 0.375),
        "weight_neigh": gaussian(key_list[2], (FEAT, FEAT), FEAT ** -0.5, 0.375),
        "norm_gain": jnp.clip(1.0 + 0.18 * jax.random.normal(key_list[3], (FEAT,), jnp.float32), 0.1, 1.9),
        "norm_shift": gaussian(key_list[4], (FEAT,), 0.5, 3.0, jnp.float32),
        "upstream": draw_upstream(jax.random.fold_in(key_list[10], 71), 0),
        "source_index": touch_ends(jax.random.randint(key_list[6], (N_ROW, N_COL, N_COL, EDGE_CAP), 0, N_ROW * NODE_DEV), jax.random.fold_in(key_list[6], 1), 0, (N_ROW * NODE_DEV) - 1).astype(jnp.int32),
        "target_index": touch_ends(jax.random.randint(key_list[7], (N_ROW, N_COL, N_COL, EDGE_CAP), 0, NODE_DEV), jax.random.fold_in(key_list[7], 1), 0, NODE_DEV - 1).astype(jnp.int32),
        "edge_weight": jnp.clip(jnp.exp(math.log(0.29882812) - 2.30176843 * jax.random.uniform(key_list[8], (N_ROW, N_COL, N_COL, EDGE_CAP), jnp.float32) ** block_levels(key_list[8], (N_ROW, N_COL, N_COL, EDGE_CAP), ((0, 8), (1, 32)), -0.2, 0.2)), 0.029907227, 0.29882812).astype(jnp.bfloat16),
        "edge_count": draw_edge_count(jax.random.fold_in(key_list[10], 71), 0),
    }


EPSILON = 1e-05

def push_rows(values, from_nodes, to_nodes, weights):

    def accumulate(tile, running):
        picked = values[from_nodes[tile]].astype(jnp.float32) * weights[tile][:, None]
        return running.at[to_nodes[tile]].add(picked)
    return lax.fori_loop(0, from_nodes.shape[0], accumulate, jnp.zeros((NODES, FEAT), jnp.float32))

def reference(features, weight_self, weight_neigh, norm_gain, norm_shift, upstream, source_index, target_index, edge_weight, edge_count):
    grid_rows = N_ROW
    grid_cols = N_COL
    slot_ids = jnp.arange(EDGE_CAP, dtype=jnp.int32)
    slot_live = slot_ids[None, None, None, :] < edge_count[..., None]
    weights = jnp.where(slot_live, edge_weight.astype(jnp.float32), jnp.zeros((), jnp.float32))
    grid_row = jnp.arange(grid_rows, dtype=jnp.int32)[:, None, None, None]
    grid_col = jnp.arange(grid_cols, dtype=jnp.int32)[None, :, None, None]
    block_ids = jnp.arange(grid_cols, dtype=jnp.int32)[None, None, :, None]
    source_node = source_index // NODE_DEV * (grid_cols * NODE_DEV) + grid_col * NODE_DEV + source_index % NODE_DEV
    target_node = (grid_row * grid_cols + block_ids) * NODE_DEV + target_index
    tiles = grid_rows * grid_cols
    source_flat = source_node.reshape(tiles, grid_cols * EDGE_CAP).astype(jnp.int32)
    target_flat = target_node.reshape(tiles, grid_cols * EDGE_CAP).astype(jnp.int32)
    weight_flat = weights.reshape(tiles, grid_cols * EDGE_CAP)
    aggregate = push_rows(features, source_flat, target_flat, weight_flat)
    mixed = aggregate.astype(jnp.bfloat16)
    hidden = jnp.dot(features, weight_self, preferred_element_type=jnp.float32) + jnp.dot(mixed, weight_neigh, preferred_element_type=jnp.float32)
    col_mean = lax.optimization_barrier(jnp.mean(hidden, axis=0))
    col_var = lax.optimization_barrier(jnp.mean((hidden - col_mean) ** 2, axis=0))
    inv_std = 1.0 / jnp.sqrt(col_var + EPSILON)
    normed = (hidden - col_mean) * inv_std
    scaled = norm_gain * normed + norm_shift
    sigmoid = jax.nn.sigmoid(scaled)
    grad_z = upstream.astype(jnp.float32) * sigmoid * (1.0 + scaled * (1.0 - sigmoid))
    sum_z = lax.optimization_barrier(jnp.sum(grad_z, axis=0))
    sum_zn = lax.optimization_barrier(jnp.sum(grad_z * normed, axis=0))
    root = math.sqrt(NODES)
    grad_shift = sum_z / root
    grad_gain = sum_zn / root
    grad_h = (norm_gain * inv_std * (grad_z - sum_z / NODES - normed * (sum_zn / NODES))).astype(jnp.bfloat16)
    grad_w_self = jnp.dot(features.T, grad_h, preferred_element_type=jnp.float32) / root
    grad_w_neigh = jnp.dot(mixed.T, grad_h, preferred_element_type=jnp.float32) / root
    grad_m = jnp.dot(grad_h, weight_neigh.T, preferred_element_type=jnp.float32).astype(jnp.bfloat16)
    back = push_rows(grad_m, target_flat, source_flat, weight_flat)
    grad_x = (jnp.dot(grad_h, weight_self.T, preferred_element_type=jnp.float32) + back).astype(jnp.bfloat16)
    return (grad_x, grad_w_self, grad_w_neigh, grad_gain, grad_shift)
```

```python
import math

import jax
import jax.numpy as jnp
from jax import lax
from jax.experimental import pallas as pl
from jax.experimental.pallas import tpu as pltpu
from jax.sharding import Mesh
from jax.sharding import PartitionSpec as P

EPSILON = 1e-05
BF = jnp.bfloat16
F32 = jnp.float32
NX, NC, NY, NZ = 4, 2, 4, 8
ALL = ("x", "c", "y", "z")
BLK = 256
VMEM = pl.BlockSpec(memory_space=pltpu.VMEM)
SMEM = pl.BlockSpec(memory_space=pltpu.SMEM)
PARAMS = pltpu.CompilerParams(vmem_limit_bytes=48 * 2**20)


def iota_bf(shape, dim):
    return lax.broadcasted_iota(jnp.int32, shape, dim).astype(F32).astype(BF)


def one_hot(iota, index, value):
    return jnp.where(iota == index, value, jnp.zeros((), BF))


def forward_kernel(x_ref, edge_ref, out_ref, picked_ref):
    lane = iota_bf((BLK, BLK), 1)
    sub = iota_bf((BLK, BLK), 0)
    one = jnp.ones((), BF)

    def dest(z, carry):
        scatter = []
        for y in range(NY):
            tile = edge_ref[y * NZ + z]
            cols = tile.T
            low = one_hot(lane, cols[:, 0:1].astype(BF), one)
            high = cols[:, 1:2]
            select = jnp.concatenate(
                [low * jnp.where(high == float(h), 1.0, 0.0).astype(BF) for h in range(NX * NC)],
                axis=1,
            )
            rows = x_ref[y * NX * NC : (y + 1) * NX * NC].reshape(NX * NC * BLK, BLK)
            picked = jnp.dot(select, rows, preferred_element_type=F32)
            picked_ref[y * BLK : (y + 1) * BLK] = picked.astype(BF)
            scatter.append(one_hot(sub, tile[2:3].astype(BF), tile[3:4].astype(BF)))
        out = jnp.dot(
            jnp.concatenate(scatter, axis=1), picked_ref[...], preferred_element_type=F32
        )
        out_ref[z] = out.astype(BF)
        return carry

    lax.fori_loop(0, NZ, dest, 0)


def backward_kernel(core_ref, grad_ref, edge_ref, send_ref, keep_ref, picked_ref, weight_ref):
    lane = iota_bf((BLK, BLK), 1)
    sub = iota_bf((BLK, BLK), 0)
    one = jnp.ones((), BF)
    core = core_ref[0].astype(F32)

    def source(y, carry):
        highs = []
        for z in range(NZ):
            tile = edge_ref[y * NZ + z]
            cols = tile.T
            gather = one_hot(lane, cols[:, 2:3].astype(BF), one)
            picked = jnp.dot(gather, grad_ref[z], preferred_element_type=F32)
            picked_ref[z * BLK : (z + 1) * BLK] = picked.astype(BF)
            weight_ref[:, z * BLK : (z + 1) * BLK] = one_hot(
                sub, tile[0:1].astype(BF), tile[3:4].astype(BF)
            )
            highs.append(tile[1:2])
        high = jnp.concatenate(highs, axis=1)
        for x in range(NX):
            for ref, part in ((send_ref, 1.0 - core), (keep_ref, core)):
                mask = jnp.where(high == 2.0 * x + part, 1.0, 0.0).astype(BF)
                out = jnp.dot(
                    weight_ref[...] * mask, picked_ref[...], preferred_element_type=F32
                )
                ref[y * NX + x] = out.astype(ref.dtype)
        return carry

    lax.fori_loop(0, NY, source, 0)


def exchange(value, axes):
    return lax.all_to_all(value, axes, 0, 0, tiled=False)


def everywhere(value, axes, count):
    return exchange(jnp.broadcast_to(value[None], (count,) + value.shape), axes)


def merge(mean, spread, rows):
    total = jnp.mean(mean, axis=0)
    moved = jnp.sum((mean - total) ** 2, axis=0)
    return total, jnp.sum(spread, axis=0) + rows * moved


def silu_parts(hidden, mean, inv_std, gain, shift, upstream):
    normed = (hidden - mean) * inv_std
    scaled = gain * normed + shift
    sigmoid = jax.nn.sigmoid(scaled)
    grad_z = upstream.astype(F32) * sigmoid * (1.0 + scaled * (1.0 - sigmoid))
    return normed, grad_z


def body(
    features,
    weight_self,
    weight_neigh,
    norm_gain,
    norm_shift,
    upstream,
    source_index,
    target_index,
    edge_weight,
    edge_count,
):
    node_total = BLK * NX * NC * NY * NZ
    root = math.sqrt(node_total)
    core = lax.axis_index("c").astype(jnp.int32).reshape(1)

    gathered = lax.all_gather(features, ("y", "x", "c"), axis=0, tiled=False)
    gathered = gathered.reshape(NY * NX * NC, BLK, BLK)
    pair = jnp.stack([features, upstream])
    pair_all = lax.all_gather(pair, "z", axis=0, tiled=False)

    source = source_index[0, 0]
    counts = edge_count[0, 0]
    slot = lax.broadcasted_iota(jnp.int32, source.shape, 1)
    weight = jnp.where(slot < counts[:, None], edge_weight[0, 0], jnp.zeros((), BF))
    edges = jnp.stack(
        [
            (source % BLK).astype(F32).astype(BF),
            (source // BLK).astype(F32).astype(BF),
            target_index[0, 0].astype(F32).astype(BF),
            weight,
        ],
        axis=1,
    )
    edges = exchange(edges.reshape(NY, NZ * 4, BLK), "y").astype(F32)
    edges = edges.reshape(NY * NZ, 4, BLK)
    edges = jnp.concatenate([edges, jnp.zeros_like(edges)], axis=1)

    partial = pl.pallas_call(
        forward_kernel,
        out_shape=jax.ShapeDtypeStruct((NZ, BLK, BLK), BF),
        in_specs=[VMEM, VMEM],
        out_specs=VMEM,
        scratch_shapes=[pltpu.VMEM((NY * BLK, BLK), BF)],
        compiler_params=PARAMS,
        name="forward_edges",
    )(gathered, edges)
    aggregate = jnp.sum(exchange(partial, "z").astype(F32), axis=0)
    mixed = aggregate.astype(BF)
    mixed_all = lax.all_gather(mixed, "z", axis=0, tiled=True)

    hidden = jnp.dot(features, weight_self, preferred_element_type=F32) + jnp.dot(
        mixed, weight_neigh, preferred_element_type=F32
    )
    mean = jnp.mean(hidden, axis=0)
    spread = jnp.sum((hidden - mean) ** 2, axis=0)
    got = everywhere(jnp.stack([mean, spread]), ("x", "c"), NX * NC)
    mean, spread = merge(got[:, 0], got[:, 1], BLK)
    got = everywhere(jnp.stack([mean, spread]), ("y", "z"), NY * NZ)
    col_mean, spread = merge(got[:, 0], got[:, 1], BLK * NX * NC)
    inv_std = lax.rsqrt(spread / node_total + EPSILON)

    normed, grad_z = silu_parts(hidden, col_mean, inv_std, norm_gain, norm_shift, upstream)
    sums = jnp.stack([jnp.sum(grad_z, axis=0), jnp.sum(grad_z * normed, axis=0)])
    sums = jnp.sum(everywhere(sums, ("x", "c"), NX * NC), axis=0)
    sums = jnp.sum(everywhere(sums, ("y", "z"), NY * NZ), axis=0)
    sum_z, sum_zn = sums[0], sums[1]
    grad_shift = sum_z / root
    grad_gain = sum_zn / root

    scale = norm_gain * inv_std
    mean_z, mean_zn = sum_z / node_total, sum_zn / node_total
    grad_h = (scale * (grad_z - mean_z - normed * mean_zn)).astype(BF)

    features_all = pair_all[:, 0].reshape(NZ * BLK, BLK)
    upstream_all = pair_all[:, 1].reshape(NZ * BLK, BLK)
    hidden_all = jnp.dot(features_all, weight_self, preferred_element_type=F32) + jnp.dot(
        mixed_all, weight_neigh, preferred_element_type=F32
    )
    normed_all, grad_z_all = silu_parts(
        hidden_all, col_mean, inv_std, norm_gain, norm_shift, upstream_all
    )
    grad_h_all = (scale * (grad_z_all - mean_z - normed_all * mean_zn)).astype(BF)
    grad_m = jnp.einsum(
        "ng,fg->nf", grad_h_all, weight_neigh, preferred_element_type=F32
    ).astype(BF)

    half = jax.ShapeDtypeStruct((NY * NX, BLK, BLK), BF)
    send, keep = pl.pallas_call(
        backward_kernel,
        out_shape=(half, half),
        in_specs=[SMEM, VMEM, VMEM],
        out_specs=(VMEM, VMEM),
        scratch_shapes=[pltpu.VMEM((NZ * BLK, BLK), BF), pltpu.VMEM((BLK, NZ * BLK), BF)],
        compiler_params=PARAMS,
        name="backward_edges",
    )(core, grad_m.reshape(NZ, BLK, BLK), edges)
    other = lax.ppermute(send, "c", [(0, 1), (1, 0)])
    both = (keep.astype(F32) + other.astype(F32)).astype(BF)
    back = jnp.sum(exchange(both, ("y", "x")).astype(F32), axis=0)
    own_term = jnp.einsum("ng,fg->nf", grad_h, weight_self, preferred_element_type=F32)
    grad_x = (own_term + back).astype(BF)

    inputs = jnp.concatenate([features, mixed], axis=1)
    term = jnp.einsum("nf,ng->fg", inputs, grad_h, preferred_element_type=F32)
    devices = NX * NC * NY * NZ
    term = exchange(term.reshape(devices, 2 * BLK // devices, BLK), ALL)
    term = jnp.sum(term, axis=0) / root
    whole = everywhere(term, ALL, devices).reshape(2 * BLK, BLK)
    return (grad_x, whole[:BLK], whole[BLK:], grad_gain, grad_shift)


def solution(mesh):
    grid = Mesh(mesh.devices.reshape(NX, NC, NY, NZ), ALL)
    row, col = ("x", "c"), ("y", "z")
    placed = (
        P(ALL, None),
        P(),
        P(),
        P(),
        P(),
        P(ALL, None),
        P(row, col, None, None),
        P(row, col, None, None),
        P(row, col, None, None),
        P(row, col, None),
    )
    return jax.shard_map(
        body,
        mesh=grid,
        in_specs=placed,
        out_specs=(P(ALL, None), P(), P(), P(), P()),
        check_vma=False,
    )
```

```python
import functools
import math

import jax
import jax.numpy as jnp
from jax import lax
from jax.experimental import pallas as pl
from jax.experimental.pallas import tpu as pltpu
from jax.sharding import Mesh
from jax.sharding import PartitionSpec as P

EPSILON = 1e-05
BF = jnp.bfloat16
F32 = jnp.float32
NX, NC, NY, NZ = 4, 2, 4, 8
ALL = ("x", "c", "y", "z")
BLK = 256
HALF = 128
VMEM = pl.BlockSpec(memory_space=pltpu.VMEM)
SMEM = pl.BlockSpec(memory_space=pltpu.SMEM)
PARAMS = pltpu.CompilerParams(vmem_limit_bytes=20 * 2**20)
LISTS = pltpu.VMEM((NY, 4 * NZ, BLK), F32)
STEPS = ((4, 3), (5, 2), (6, 7), (1, 0))


def iota_bf(shape, dim):
    return lax.broadcasted_iota(jnp.int32, shape, dim).astype(F32).astype(BF)


def one_hot(iota, index, value):
    return jnp.where(iota == index, value, jnp.zeros((), BF))


def read_lists(lower, list_ref):
    for y in range(NY):
        list_ref[y] = lower[y][NX * HALF :].astype(F32)


def forward_kernel(offsets, place_ref, *refs):
    upper, lower = (refs[:NX], refs[NX : 2 * NX]), (refs[2 * NX : 3 * NX], refs[3 * NX : 4 * NX])
    outs, (picked_ref, list_ref) = refs[4 * NX : -2], refs[-2:]
    lane = iota_bf((BLK, BLK), 1)
    sub = iota_bf((BLK, BLK), 0)
    one = jnp.ones((), BF)
    read_lists(lower[0], list_ref)
    for offset, out_ref in zip(offsets, outs):
        z = jnp.bitwise_xor(place_ref[0], offset)
        scatter = []
        for y in range(NY):
            low, high, target, weight = (
                list_ref[y, pl.ds(field * NZ + z, 1), :] for field in range(4)
            )
            cols = jnp.concatenate([low, high] * 4, axis=0).T
            low = one_hot(lane, cols[:, 0:1].astype(BF), one)
            high = cols[:, 1:2]
            select, rows = [], []
            for x in range(NX):
                for c in range(NC):
                    mask = jnp.where(high == float(x * NC + c), 1.0, 0.0).astype(BF)
                    select.append(low * mask)
                    rows += [upper[c][x][y], lower[c][y][x * HALF : (x + 1) * HALF]]
            picked = jnp.dot(
                jnp.concatenate(select, axis=1),
                jnp.concatenate(rows, axis=0),
                preferred_element_type=F32,
            )
            picked_ref[y * BLK : (y + 1) * BLK] = picked.astype(BF)
            scatter.append(one_hot(sub, target.astype(BF), weight.astype(BF)))
        out = jnp.dot(
            jnp.concatenate(scatter, axis=1), picked_ref[...], preferred_element_type=F32
        )
        out_ref[...] = out.astype(BF)


def backward_kernel(grad_ref, *refs):
    lower, (keep_ref, send_ref, picked_ref, weight_ref, list_ref) = refs[:NY], refs[NY:]
    lane = iota_bf((BLK, BLK), 1)
    sub = iota_bf((BLK, BLK), 0)
    one = jnp.ones((), BF)
    read_lists(lower, list_ref)

    def source(y, carry):
        lists = list_ref[y]
        cols = lists[2 * NZ : 3 * NZ].T
        highs = []
        for z in range(NZ):
            low, high, weight = (lists[f * NZ + z : f * NZ + z + 1] for f in (0, 1, 3))
            gather = one_hot(lane, cols[:, z : z + 1].astype(BF), one)
            picked = jnp.dot(gather, grad_ref[z], preferred_element_type=F32)
            picked_ref[z * BLK : (z + 1) * BLK] = picked.astype(BF)
            weight_ref[:, z * BLK : (z + 1) * BLK] = one_hot(
                sub, low.astype(BF), weight.astype(BF)
            )
            highs.append(high)
        high = jnp.concatenate(highs, axis=1)
        for x in range(NX):
            for ref, c in ((keep_ref, 0), (send_ref, 1)):
                mask = jnp.where(high == float(x * NC + c), 1.0, 0.0).astype(BF)
                out = jnp.dot(
                    weight_ref[...] * mask, picked_ref[...], preferred_element_type=F32
                ).astype(BF)
                ref[0, x * NY + y] = out[:HALF]
                ref[1, y * NX + x] = out[HALF:]
        return carry

    lax.fori_loop(0, NY, source, 0)


def swap(value, axis, offset):
    count = {"x": NX, "c": NC, "y": NY, "z": NZ}[axis]
    return lax.ppermute(value, axis, [(i, i ^ offset) for i in range(count)])


def spread_out(value, axis):
    return [value] + [swap(value, axis, k) for k in (1, 2, 3)]


def reduce_in(value, axis):
    got = [swap(value[k], axis, k) for k in (2, 1, 3)]
    return value[0].astype(F32) + sum(part.astype(F32) for part in got)


def exchange(value, axes):
    return lax.all_to_all(value, axes, 0, 0, tiled=False)


def everywhere(value, axes, count):
    return exchange(jnp.broadcast_to(value[None], (count,) + value.shape), axes)


def merge(mean, spread, rows):
    total = jnp.mean(mean, axis=0)
    moved = jnp.sum((mean - total) ** 2, axis=0)
    return total, jnp.sum(spread, axis=0) + rows * moved


def silu_parts(hidden, mean, inv_std, gain, shift, upstream):
    normed = (hidden - mean) * inv_std
    scaled = gain * normed + shift
    sigmoid = jax.nn.sigmoid(scaled)
    grad_z = upstream.astype(F32) * sigmoid * (1.0 + scaled * (1.0 - sigmoid))
    return normed, grad_z


def body(
    features,
    weight_self,
    weight_neigh,
    norm_gain,
    norm_shift,
    upstream,
    source_index,
    target_index,
    edge_weight,
    edge_count,
):
    node_total = BLK * NX * NC * NY * NZ
    root = math.sqrt(node_total)
    place = lax.axis_index("y").astype(jnp.int32)
    place_z = lax.axis_index("z").astype(jnp.int32)
    own = lax.axis_index("x") * NC + lax.axis_index("c")

    source = source_index[0, 0]
    counts = edge_count[0, 0]
    slot = lax.broadcasted_iota(jnp.int32, source.shape, 1)
    weight = jnp.where(slot < counts[:, None], edge_weight[0, 0], jnp.zeros((), BF))
    edges = jnp.stack(
        [
            (source % BLK).astype(F32).astype(BF),
            jnp.bitwise_xor(source // BLK, own).astype(F32).astype(BF),
            target_index[0, 0].astype(F32).astype(BF),
            weight,
        ]
    )
    edges = edges.reshape(4, NY, NZ, BLK).swapaxes(0, 1).reshape(NY, 4 * NZ, BLK)

    pair = jnp.stack([features, upstream])
    pair_all = lax.all_gather(pair, "z", axis=0, tiled=False)

    upper = spread_out(jnp.stack(spread_out(features[:HALF], "y")), "x")
    lower = spread_out(features[HALF:], "x")
    for k in range(NY):
        lists = lax.dynamic_index_in_dim(edges, jnp.bitwise_xor(place, k), 0, keepdims=False)
        half = jnp.concatenate(lower[:NX] + [lists], axis=0)
        lower.append(swap(half, "y", k) if k else half)
    lower = lower[NX:]
    sources = upper + [swap(part, "c", 1) for part in upper]
    sources += lower + [swap(part, "c", 1) for part in lower]
    sources, pair_all = lax.optimization_barrier((sources, pair_all))

    block = jax.ShapeDtypeStruct((BLK, BLK), BF)
    aggregate = jnp.zeros((BLK, BLK), F32)
    for offsets in STEPS:
        partial = pl.pallas_call(
            functools.partial(forward_kernel, offsets),
            out_shape=(block, block),
            in_specs=[SMEM] + [VMEM] * len(sources),
            out_specs=(VMEM, VMEM),
            scratch_shapes=[pltpu.VMEM((NY * BLK, BLK), BF), LISTS],
            compiler_params=PARAMS,
            cost_estimate=pl.CostEstimate(
                flops=4 * 10**9, bytes_accessed=5 * 2**20, transcendentals=0
            ),
            name="forward_edges",
        )(place_z.reshape(1), *sources)
        for offset, part in zip(offsets, partial):
            part = swap(part, "z", offset) if offset else part
            aggregate = aggregate + part.astype(F32)
    mixed = aggregate.astype(BF)
    mixed_all = lax.all_gather(mixed, "z", axis=0, tiled=True)

    hidden = jnp.dot(features, weight_self, preferred_element_type=F32) + jnp.dot(
        mixed, weight_neigh, preferred_element_type=F32
    )
    mean = jnp.mean(hidden, axis=0)
    spread = jnp.sum((hidden - mean) ** 2, axis=0)
    got = everywhere(jnp.stack([mean, spread]), ("x", "c"), NX * NC)
    mean, spread = merge(got[:, 0], got[:, 1], BLK)
    got = everywhere(jnp.stack([mean, spread]), ("y", "z"), NY * NZ)
    col_mean, spread = merge(got[:, 0], got[:, 1], BLK * NX * NC)
    inv_std = lax.rsqrt(spread / node_total + EPSILON)

    features_all = pair_all[:, 0].reshape(NZ * BLK, BLK)
    upstream_all = pair_all[:, 1].reshape(NZ * BLK, BLK)
    hidden_all = jnp.dot(features_all, weight_self, preferred_element_type=F32) + jnp.dot(
        mixed_all, weight_neigh, preferred_element_type=F32
    )
    normed_all, grad_z_all = silu_parts(
        hidden_all, col_mean, inv_std, norm_gain, norm_shift, upstream_all
    )
    sums = jnp.stack(
        [jnp.sum(grad_z_all, axis=0), jnp.sum(grad_z_all * normed_all, axis=0)]
    )
    sums = jnp.sum(everywhere(sums, ("x", "c", "y"), NX * NC * NY), axis=0)
    sum_z, sum_zn = sums[0], sums[1]
    grad_shift = sum_z / root
    grad_gain = sum_zn / root

    scale = norm_gain * inv_std
    mean_z, mean_zn = sum_z / node_total, sum_zn / node_total
    grad_h_all = (scale * (grad_z_all - mean_z - normed_all * mean_zn)).astype(BF)
    grad_m = jnp.einsum(
        "ng,fg->nf", grad_h_all, weight_neigh, preferred_element_type=F32
    ).astype(BF)

    half = jax.ShapeDtypeStruct((2, NX * NY, HALF, BLK), BF)
    keep, send = pl.pallas_call(
        backward_kernel,
        out_shape=(half, half),
        in_specs=[VMEM] * (1 + NY),
        out_specs=(VMEM, VMEM),
        scratch_shapes=[
            pltpu.VMEM((NZ * BLK, BLK), BF),
            pltpu.VMEM((BLK, NZ * BLK), BF),
            LISTS,
        ],
        compiler_params=PARAMS,
        cost_estimate=pl.CostEstimate(
            flops=16 * 10**9, bytes_accessed=6 * 2**20, transcendentals=0
        ),
        name="backward_edges",
    )(grad_m.reshape(NZ, BLK, BLK), *lower)
    other = swap(send, "c", 1)
    both = [
        [
            (keep[h, k * 4 : k * 4 + 4].astype(F32) + other[h, k * 4 : k * 4 + 4].astype(F32))
            for k in range(4)
        ]
        for h in range(2)
    ]
    both = [[part.astype(BF) for part in parts] for parts in both]
    term = [
        jnp.einsum("nf,ng->fg", rows, grad_h_all, preferred_element_type=F32)
        for rows in (features_all, mixed_all)
    ]
    term = jnp.concatenate(term, axis=0).reshape(NZ, 2 * BLK // NZ, BLK)
    term = lax.dynamic_index_in_dim(term, place_z, axis=0, keepdims=False)
    both, term = lax.optimization_barrier((both, term))
    upper = reduce_in(reduce_in(both[0], "x").astype(BF), "y")
    lower = reduce_in(reduce_in(both[1], "y").astype(BF), "x")
    back = jnp.concatenate([upper, lower], axis=0)
    grad_h = lax.dynamic_index_in_dim(
        grad_h_all.reshape(NZ, BLK, BLK), place_z, axis=0, keepdims=False
    )
    own_term = jnp.einsum("ng,fg->nf", grad_h, weight_self, preferred_element_type=F32)
    grad_x = (own_term + back).astype(BF)

    group = NX * NC * NY
    term = exchange(term.reshape(group, 2 * BLK // NZ // group, BLK), ("x", "c", "y"))
    term = jnp.sum(term, axis=0) / root
    whole = everywhere(term, ("z", "x", "c", "y"), NZ * group).reshape(2 * BLK, BLK)
    return (grad_x, whole[:BLK], whole[BLK:], grad_gain, grad_shift)


def solution(mesh):
    grid = Mesh(mesh.devices.reshape(NX, NC, NY, NZ), ALL)
    row, col = ("x", "c"), ("y", "z")
    placed = (
        P(ALL, None),
        P(),
        P(),
        P(),
        P(),
        P(ALL, None),
        P(row, col, None, None),
        P(row, col, None, None),
        P(row, col, None, None),
        P(row, col, None),
    )
    return jax.shard_map(
        body,
        mesh=grid,
        in_specs=placed,
        out_specs=(P(ALL, None), P(), P(), P(), P()),
        check_vma=False,
    )
```

```python
import functools
import math

import jax
import jax.numpy as jnp
from jax import lax
from jax.experimental import pallas as pl
from jax.experimental.pallas import tpu as pltpu
from jax.sharding import Mesh
from jax.sharding import PartitionSpec as P

EPSILON = 1e-05
BF = jnp.bfloat16
F32 = jnp.float32
NX, NC, NY, NZ = 4, 2, 4, 8
ALL = ("x", "c", "y", "z")
BLK = 256
HALF = 128
GROUP = NX * NC * NY
ROWS = 2 * BLK // NZ
VMEM = pl.BlockSpec(memory_space=pltpu.VMEM)
SMEM = pl.BlockSpec(memory_space=pltpu.SMEM)
PARAMS = pltpu.CompilerParams(vmem_limit_bytes=12 * 2**20)
LISTS = pltpu.VMEM((NY, 4 * NZ, BLK), F32)
STEPS = ((4, 1), (5, 2), (7, 3), (6, 0))
WAITS = ((), (), (1,), (4, 2))


def iota_bf(shape, dim):
    return lax.broadcasted_iota(jnp.int32, shape, dim).astype(F32).astype(BF)


def one_hot(iota, index, value):
    return jnp.where(iota == index, value, jnp.zeros((), BF))


def read_lists(lower, list_ref):
    for y in range(NY):
        list_ref[y] = lower[y, NX * HALF :].astype(F32)


def forward_kernel(offsets, place_ref, *refs):
    upper, lower = refs[:2], refs[2:4]
    outs, (picked_ref, list_ref) = refs[4:-2], refs[-2:]
    lane = iota_bf((BLK, BLK), 1)
    sub = iota_bf((BLK, BLK), 0)
    one = jnp.ones((), BF)
    read_lists(lower[0], list_ref)
    for offset, out_ref in zip(offsets, outs):
        z = jnp.bitwise_xor(place_ref[0], offset)
        scatter = []
        for y in range(NY):
            low, high, target, weight = (
                list_ref[y, pl.ds(field * NZ + z, 1), :] for field in range(4)
            )
            cols = jnp.concatenate([low, high] * 4, axis=0).T
            low = one_hot(lane, cols[:, 0:1].astype(BF), one)
            high = cols[:, 1:2]
            select, rows = [], []
            for x in range(NX):
                for c in range(NC):
                    mask = jnp.where(high == float(x * NC + c), 1.0, 0.0).astype(BF)
                    select.append(low * mask)
                    rows += [upper[c][x, y], lower[c][y, x * HALF : (x + 1) * HALF]]
            picked = jnp.dot(
                jnp.concatenate(select, axis=1),
                jnp.concatenate(rows, axis=0),
                preferred_element_type=F32,
            )
            picked_ref[y * BLK : (y + 1) * BLK] = picked.astype(BF)
            scatter.append(one_hot(sub, target.astype(BF), weight.astype(BF)))
        out = jnp.dot(
            jnp.concatenate(scatter, axis=1), picked_ref[...], preferred_element_type=F32
        )
        out_ref[...] = out.astype(BF)


def stats_kernel(place_ref, self_ref, neigh_ref, pair_ref, *refs):
    mixed, stats_ref, hidden_refs = refs[:NZ], refs[NZ], refs[NZ + 1 :]
    parts = []
    for k in range(NZ):
        z = jnp.bitwise_xor(place_ref[0], k)
        hidden = jnp.dot(pair_ref[z, 0], self_ref[...], preferred_element_type=F32)
        hidden += jnp.dot(mixed[k][...], neigh_ref[...], preferred_element_type=F32)
        hidden_refs[k][...] = hidden
        mean = jnp.sum(hidden, axis=0, keepdims=True) * (1.0 / BLK)
        parts.append((mean, jnp.sum((hidden - mean) ** 2, axis=0, keepdims=True)))
    rows = BLK
    while len(parts) > 1:
        parts = [
            ((m0 + m1) * 0.5, s0 + s1 + (0.5 * rows) * (m0 - m1) ** 2)
            for (m0, s0), (m1, s1) in zip(parts[::2], parts[1::2])
        ]
        rows *= 2
    stats_ref[...] = jnp.concatenate(parts[0], axis=0)


def group_kernel(place_ref, vec_ref, pair_ref, *refs):
    mixed, hidden, payload_ref = refs[:NZ], refs[NZ : 2 * NZ], refs[2 * NZ]
    grad_refs, normed_refs = refs[2 * NZ + 1 : 3 * NZ + 1], refs[3 * NZ + 1 : 4 * NZ + 1]
    left_ref, right_ref, prod_ref = refs[4 * NZ + 1 :]
    mean, inv_std, gain, shift = (vec_ref[i : i + 1] for i in range(4))
    sums = []
    for k in range(NZ):
        z = jnp.bitwise_xor(place_ref[0], k)
        left_ref[k * BLK : (k + 1) * BLK, :BLK] = pair_ref[z, 0]
        left_ref[k * BLK : (k + 1) * BLK, BLK:] = mixed[k][...]
        normed, grad_z = silu_parts(hidden[k][...], mean, inv_std, gain, shift, pair_ref[z, 1])
        grad_refs[k][...] = grad_z
        normed_refs[k][...] = normed
        sums.append(
            jnp.concatenate(
                [
                    jnp.sum(grad_z, axis=0, keepdims=True),
                    jnp.sum(grad_z * normed, axis=0, keepdims=True),
                ],
                axis=0,
            )
        )
        for i, value in enumerate((grad_z, normed)):
            big = value.astype(BF)
            small = (value - big.astype(F32)).astype(BF)
            right_ref[k * BLK : (k + 1) * BLK, 2 * i * BLK : (2 * i + 1) * BLK] = big
            right_ref[k * BLK : (k + 1) * BLK, (2 * i + 1) * BLK : (2 * i + 2) * BLK] = small
    right_ref[:, 4 * BLK :] = jnp.ones((NZ * BLK, HALF), BF)
    while len(sums) > 1:
        sums = [sums[i] + sums[i + 1] for i in range(0, len(sums), 2)]
    prod_ref[...] = lax.dot_general(
        left_ref[...], right_ref[...], (((0,), (0,)), ((), ())), preferred_element_type=F32
    )
    mine = prod_ref[pl.ds(pl.multiple_of(place_ref[0] * ROWS, ROWS), ROWS), :]
    with_z = mine[:, :BLK] + mine[:, BLK : 2 * BLK]
    with_n = mine[:, 2 * BLK : 3 * BLK] + mine[:, 3 * BLK : 4 * BLK]
    count = mine[:, 4 * BLK :]
    count = jnp.concatenate([count, count], axis=1)
    for i in range(GROUP):
        part = slice(2 * i, 2 * i + 2)
        payload_ref[i] = jnp.concatenate(
            [sums[0], with_z[part], with_n[part], count[part]], axis=0
        )


def backward_kernel(core, half, place_ref, grad, lower, outs, picked_ref, weight_ref, list_ref):
    lane = iota_bf((BLK, BLK), 1)
    tall = BLK if half is None else HALF
    sub = lax.broadcasted_iota(jnp.int32, (tall, BLK), 0) + HALF * (half or 0)
    sub = sub.astype(F32).astype(BF)
    one = jnp.ones((), BF)
    read_lists(lower, list_ref)
    for y in range(NY):
        lists = []
        for k in range(NZ):
            z = jnp.bitwise_xor(place_ref[0], k)
            lists.append([list_ref[y, pl.ds(field * NZ + z, 1), :] for field in range(4)])
        cols = jnp.concatenate([row[2] for row in lists], axis=0).T
        for k in range(NZ):
            gather = one_hot(lane, cols[:, k : k + 1].astype(BF), one)
            picked = jnp.dot(gather, grad[k], preferred_element_type=F32)
            picked_ref[k * BLK : (k + 1) * BLK] = picked.astype(BF)
            weight_ref[:, k * BLK : (k + 1) * BLK] = one_hot(
                sub, lists[k][0].astype(BF), lists[k][3].astype(BF)
            )
        high = jnp.concatenate([row[1] for row in lists], axis=1)
        step = 1 if half is None else 2
        for x in range(0, NX, step):
            left = [
                weight_ref[...] * jnp.where(high == float(i * NC + core), 1.0, 0.0).astype(BF)
                for i in range(x, x + step)
            ]
            left = left[0] if half is None else jnp.concatenate(left, axis=0)
            out = jnp.dot(left, picked_ref[...], preferred_element_type=F32).astype(BF)
            if half is None:
                outs[0, x * NY + y], outs[1, y * NX + x] = out[:HALF], out[HALF:]
            else:
                for i in range(step):
                    part = out[i * HALF : (i + 1) * HALF]
                    if half:
                        outs[y][x + i] = part
                    else:
                        outs[x + i][y] = part


def totals_kernel(got_ref, vec_ref, out_ref, vec2_ref, term_ref):
    total = got_ref[0]
    for i in range(1, GROUP):
        total = total + got_ref[i]
    root = math.sqrt(GROUP * NZ * BLK)
    scale = vec_ref[1:2] * vec_ref[2:3]
    out_ref[...] = total[:2] * (1.0 / root)
    means = total[:2] * (1.0 / (GROUP * NZ * BLK))
    vec2_ref[...] = jnp.concatenate([scale, means, scale], axis=0)
    term = total[2:4] - total[6:8] * means[0:1] - total[4:6] * means[1:2]
    term_ref[...] = scale * term * (1.0 / root)


def send_kernel(place_ref, vec_ref, self_ref, neigh_ref, lower, *refs):
    grad_z, normed = refs[:NZ], refs[NZ : 2 * NZ]
    send_ref, own_ref, grad_m = refs[2 * NZ : 2 * NZ + 3]
    scale, mean_z, mean_zn = (vec_ref[i : i + 1] for i in range(3))
    for k in range(NZ):
        grad_h = scale * (grad_z[k][...] - mean_z - normed[k][...] * mean_zn)
        grad_h = grad_h.astype(BF)
        grad_m[k] = lax.dot_general(
            grad_h, neigh_ref[...], (((1,), (1,)), ((), ())), preferred_element_type=F32
        ).astype(BF)
        if k == 0:
            own_ref[...] = lax.dot_general(
                grad_h, self_ref[...], (((1,), (1,)), ((), ())), preferred_element_type=F32
            )
    backward_kernel(1, None, place_ref, grad_m, lower, send_ref, *refs[2 * NZ + 3 :])


def keep_kernel(half, place_ref, lower, grad_m, *refs):
    backward_kernel(0, half, place_ref, grad_m, lower, refs[:4], *refs[4:])


def swap(value, axis, offset):
    count = {"x": NX, "c": NC, "y": NY, "z": NZ}[axis]
    return lax.ppermute(value, axis, [(i, i ^ offset) for i in range(count)])


def spread_out(value, axis):
    return [value] + [swap(value, axis, k) for k in (1, 2, 3)]


def reduce_in(value, axis):
    got = [swap(value[k], axis, k) for k in (2, 1, 3)]
    return value[0].astype(F32) + sum(part.astype(F32) for part in got)


def exchange(value, axes):
    return lax.all_to_all(value, axes, 0, 0, tiled=False)


def everywhere(value, axes, count):
    return exchange(jnp.broadcast_to(value[None], (count,) + value.shape), axes)


def merge(mean, spread, rows):
    total = jnp.mean(mean, axis=0)
    moved = jnp.sum((mean - total) ** 2, axis=0)
    return total, jnp.sum(spread, axis=0) + rows * moved


def silu_parts(hidden, mean, inv_std, gain, shift, upstream):
    normed = (hidden - mean) * inv_std
    scaled = gain * normed + shift
    sigmoid = jax.nn.sigmoid(scaled)
    grad_z = upstream.astype(F32) * sigmoid * (1.0 + scaled * (1.0 - sigmoid))
    return normed, grad_z


def body(
    features,
    weight_self,
    weight_neigh,
    norm_gain,
    norm_shift,
    upstream,
    source_index,
    target_index,
    edge_weight,
    edge_count,
):
    node_total = BLK * NX * NC * NY * NZ
    root = math.sqrt(node_total)
    place = lax.axis_index("y").astype(jnp.int32)
    place_z = lax.axis_index("z").astype(jnp.int32).reshape(1)
    own = lax.axis_index("x") * NC + lax.axis_index("c")

    pair = jnp.stack([features, upstream])
    turns = [jnp.bitwise_xor(place, k) for k in range(NY)]
    near, pair, turns, place_z, own = lax.optimization_barrier(
        (features, pair, turns, place_z, own)
    )

    source = source_index[0, 0]
    counts = edge_count[0, 0]
    slot = lax.broadcasted_iota(jnp.int32, source.shape, 1)
    weight = jnp.where(slot < counts[:, None], edge_weight[0, 0], jnp.zeros((), BF))
    edges = jnp.stack(
        [
            (source % BLK).astype(F32).astype(BF),
            jnp.bitwise_xor(source // BLK, own).astype(F32).astype(BF),
            target_index[0, 0].astype(F32).astype(BF),
            weight,
        ]
    )
    edges = edges.reshape(4, NY, NZ, BLK).swapaxes(0, 1).reshape(NY, 4 * NZ, BLK)


    pair_all = lax.all_gather(pair, "z", axis=0, tiled=False)
    upper = jnp.stack(spread_out(jnp.stack(spread_out(near[:HALF], "y")), "x"))
    first = spread_out(near[HALF:], "x")
    lower = []
    for k in range(NY):
        lists = lax.dynamic_slice(
            edges, (turns[k], 0, 0), (1, 4 * NZ, BLK), allow_negative_indices=False
        )[0]
        half = jnp.concatenate(first + [lists], axis=0)
        lower.append(swap(half, "y", k) if k else half)
    lower = jnp.stack(lower)
    sources = [upper, swap(upper, "c", 1), lower, swap(lower, "c", 1)]

    block = jax.ShapeDtypeStruct((BLK, BLK), BF)
    parts = {}
    for offsets, waits in zip(STEPS, WAITS):
        sources, ready = lax.optimization_barrier((sources, [parts[k] for k in waits]))
        parts.update(zip(waits, ready))
        if offsets is STEPS[1]:
            sources, pair_all = lax.optimization_barrier((sources, pair_all))
        partial = pl.pallas_call(
            functools.partial(forward_kernel, offsets),
            out_shape=(block, block),
            in_specs=[SMEM] + [VMEM] * len(sources),
            out_specs=(VMEM, VMEM),
            scratch_shapes=[pltpu.VMEM((NY * BLK, BLK), BF), LISTS],
            compiler_params=PARAMS,
            cost_estimate=pl.CostEstimate(
                flops=4 * 10**9, bytes_accessed=5 * 2**20, transcendentals=0
            ),
            name="forward_edges",
        )(place_z, *sources)
        for offset, part in zip(offsets, partial):
            parts[offset] = swap(part, "z", offset) if offset else part
    lower = sources[2]
    aggregate = sum(parts[k].astype(F32) for k in range(NZ))
    mixed = aggregate.astype(BF)
    mixed_all = [mixed] + [swap(mixed, "z", k) for k in (1, 2, 6, 7, 3, 5, 4)]
    mixed_all = [mixed_all[i] for i in (0, 1, 2, 5, 7, 6, 3, 4)]

    blocks = (jax.ShapeDtypeStruct((BLK, BLK), F32),) * NZ
    stats, *hidden_all = pl.pallas_call(
        stats_kernel,
        out_shape=(jax.ShapeDtypeStruct((2, BLK), F32), *blocks),
        in_specs=[SMEM] + [VMEM] * (3 + NZ),
        out_specs=(VMEM,) * (1 + NZ),
        compiler_params=PARAMS,
        cost_estimate=pl.CostEstimate(
            flops=10**9, bytes_accessed=5 * 2**20, transcendentals=0
        ),
        name="group_stats",
    )(place_z, weight_self, weight_neigh, pair_all, *mixed_all)
    got = everywhere(stats, ("x", "c", "y"), GROUP)
    col_mean, spread = merge(got[:, 0], got[:, 1], BLK * NZ)
    inv_std = lax.rsqrt(spread / node_total + EPSILON)

    vectors = jnp.stack([col_mean, inv_std, norm_gain, norm_shift])
    payload, *grads = pl.pallas_call(
        group_kernel,
        out_shape=(jax.ShapeDtypeStruct((GROUP, 8, BLK), F32), *blocks, *blocks),
        in_specs=[SMEM] + [VMEM] * (2 + 2 * NZ),
        out_specs=(VMEM,) * (1 + 2 * NZ),
        scratch_shapes=[
            pltpu.VMEM((NZ * BLK, 2 * BLK), BF),
            pltpu.VMEM((NZ * BLK, 4 * BLK + HALF), BF),
            pltpu.VMEM((2 * BLK, 4 * BLK + HALF), F32),
        ],
        compiler_params=pltpu.CompilerParams(vmem_limit_bytes=20 * 2**20),
        cost_estimate=pl.CostEstimate(
            flops=5 * 10**9, bytes_accessed=8 * 2**20, transcendentals=0
        ),
        name="group_terms",
    )(place_z, vectors, pair_all, *mixed_all, *hidden_all)
    sums, vectors, term = pl.pallas_call(
        totals_kernel,
        out_shape=(
            jax.ShapeDtypeStruct((2, BLK), F32),
            jax.ShapeDtypeStruct((4, BLK), F32),
            jax.ShapeDtypeStruct((2, BLK), F32),
        ),
        in_specs=[VMEM, VMEM],
        out_specs=(VMEM,) * 3,
        compiler_params=PARAMS,
        name="totals",
    )(exchange(payload, ("x", "c", "y")), vectors)
    grad_shift, grad_gain = sums[0], sums[1]
    whole = everywhere(term, ("z", "x", "c", "y"), NZ * GROUP)

    scratch = [
        pltpu.VMEM((NZ * BLK, BLK), BF),
        pltpu.VMEM((BLK, NZ * BLK), BF),
        LISTS,
    ]
    cost = pl.CostEstimate(flops=8 * 10**9, bytes_accessed=6 * 2**20, transcendentals=0)
    send, own_term, grad_m = pl.pallas_call(
        send_kernel,
        out_shape=(
            jax.ShapeDtypeStruct((2, NX * NY, HALF, BLK), BF),
            jax.ShapeDtypeStruct((BLK, BLK), F32),
            jax.ShapeDtypeStruct((NZ, BLK, BLK), BF),
        ),
        in_specs=[SMEM] + [VMEM] * (4 + 2 * NZ),
        out_specs=(VMEM,) * 3,
        scratch_shapes=scratch,
        compiler_params=PARAMS,
        cost_estimate=cost,
        name="backward_send",
    )(place_z, vectors, weight_self, weight_neigh, lower, *grads)
    other = swap(send, "c", 1).reshape(2, 4, 4, HALF, BLK)
    scratch[1] = pltpu.VMEM((HALF, NZ * BLK), BF)
    both = []
    for half in range(2):
        if half:
            grad_m, both = lax.optimization_barrier((grad_m, both))
        keep = pl.pallas_call(
            functools.partial(keep_kernel, half),
            out_shape=(jax.ShapeDtypeStruct((4, HALF, BLK), BF),) * 4,
            in_specs=[SMEM] + [VMEM] * 2,
            out_specs=(VMEM,) * 4,
            scratch_shapes=scratch,
            compiler_params=PARAMS,
            cost_estimate=cost,
            name="backward_keep",
        )(place_z, lower, grad_m)
        both.append(
            [(keep[k].astype(F32) + other[half, k].astype(F32)).astype(BF) for k in range(4)]
        )
    both, whole = lax.optimization_barrier((both, whole))
    whole = [part.reshape(BLK, BLK) for part in jnp.split(whole, 2)]
    upper, whole = lax.optimization_barrier((reduce_in(both[0], "x").astype(BF), whole))
    upper = reduce_in(upper, "y")
    lower = reduce_in(reduce_in(both[1], "y").astype(BF), "x")
    back = jnp.concatenate([upper, lower], axis=0)
    grad_x = (own_term + back).astype(BF)

    return (grad_x, whole[0], whole[1], grad_gain, grad_shift)


def solution(mesh):
    grid = Mesh(mesh.devices.reshape(NX, NC, NY, NZ), ALL)
    row, col = ("x", "c"), ("y", "z")
    placed = (
        P(ALL, None),
        P(),
        P(),
        P(),
        P(),
        P(ALL, None),
        P(row, col, None, None),
        P(row, col, None, None),
        P(row, col, None, None),
        P(row, col, None),
    )
    return jax.shard_map(
        body,
        mesh=grid,
        in_specs=placed,
        out_specs=(P(ALL, None), P(), P(), P(), P()),
        check_vma=False,
    )
```

```python
import functools
import math

import jax
import jax.numpy as jnp
from jax import lax
from jax.experimental import pallas as pl
from jax.experimental.pallas import tpu as pltpu
from jax.sharding import Mesh
from jax.sharding import PartitionSpec as P

EPSILON = 1e-05
BF = jnp.bfloat16
F32 = jnp.float32
NX, NC, NY, NZ = 4, 2, 4, 8
ALL = ("x", "c", "y", "z")
BLK = 256
HALF = 128
GROUP = NX * NC * NY
ROWS = 2 * BLK // NZ
VMEM = pl.BlockSpec(memory_space=pltpu.VMEM)
SMEM = pl.BlockSpec(memory_space=pltpu.SMEM)
PARAMS = pltpu.CompilerParams(vmem_limit_bytes=12 * 2**20)
LISTS = pltpu.VMEM((NY, 4 * NZ, BLK), F32)
STEPS = ((4,), (3, 5), (2, 6), (1, 7), (0,))


def iota_bf(shape, dim):
    return lax.broadcasted_iota(jnp.int32, shape, dim).astype(F32).astype(BF)


def one_hot(iota, index, value):
    return jnp.where(iota == index, value, jnp.zeros((), BF))


def read_lists(lower, list_ref):
    for y in range(NY):
        list_ref[y] = lower[y, NX * HALF :].astype(F32)


def forward_kernel(offsets, place_ref, *refs):
    upper, lower = refs[:2], refs[2:4]
    outs, (picked_ref, list_ref) = refs[4:-2], refs[-2:]
    lane = iota_bf((BLK, BLK), 1)
    sub = iota_bf((BLK, BLK), 0)
    one = jnp.ones((), BF)
    read_lists(lower[0], list_ref)
    for offset, out_ref in zip(offsets, outs):
        z = jnp.bitwise_and(place_ref[0] + offset, NZ - 1)
        scatter = []
        for y in range(NY):
            low, high, target, weight = (
                list_ref[y, pl.ds(field * NZ + z, 1), :] for field in range(4)
            )
            cols = jnp.concatenate([low, high] * 4, axis=0).T
            low = one_hot(lane, cols[:, 0:1].astype(BF), one)
            high = cols[:, 1:2]
            select, rows = [], []
            for x in range(NX):
                for c in range(NC):
                    mask = jnp.where(high == float(x * NC + c), 1.0, 0.0).astype(BF)
                    select.append(low * mask)
                    rows += [upper[c][x, y], lower[c][y, x * HALF : (x + 1) * HALF]]
            picked = jnp.dot(
                jnp.concatenate(select, axis=1),
                jnp.concatenate(rows, axis=0),
                preferred_element_type=F32,
            )
            picked_ref[y * BLK : (y + 1) * BLK] = picked.astype(BF)
            scatter.append(one_hot(sub, target.astype(BF), weight.astype(BF)))
        out = jnp.dot(
            jnp.concatenate(scatter, axis=1), picked_ref[...], preferred_element_type=F32
        )
        out_ref[...] = out


def stats_kernel(place_ref, self_ref, neigh_ref, pair_ref, *refs):
    mixed, stats_ref, hidden_refs, part_ref = refs[:NZ], refs[NZ], refs[NZ + 1 : -1], refs[-1]
    for k in range(NZ):
        z = jnp.bitwise_and(place_ref[0] + k, NZ - 1)
        hidden = jnp.dot(pair_ref[z, 0], self_ref[...], preferred_element_type=F32)
        hidden += jnp.dot(mixed[k][...], neigh_ref[...], preferred_element_type=F32)
        hidden_refs[k][...] = hidden
        mean = jnp.sum(hidden, axis=0, keepdims=True) * (1.0 / BLK)
        part_ref[0, pl.ds(z, 1), :] = mean
        part_ref[1, pl.ds(z, 1), :] = jnp.sum((hidden - mean) ** 2, axis=0, keepdims=True)
    means, spreads = part_ref[0], part_ref[1]
    parts = [(means[z : z + 1], spreads[z : z + 1]) for z in range(NZ)]
    rows = BLK
    while len(parts) > 1:
        parts = [
            ((m0 + m1) * 0.5, s0 + s1 + (0.5 * rows) * (m0 - m1) ** 2)
            for (m0, s0), (m1, s1) in zip(parts[::2], parts[1::2])
        ]
        rows *= 2
    stats_ref[...] = jnp.concatenate(parts[0], axis=0)


def group_kernel(place_ref, vec_ref, pair_ref, *refs):
    mixed, hidden, payload_ref = refs[:NZ], refs[NZ : 2 * NZ], refs[2 * NZ]
    grad_refs, normed_refs = refs[2 * NZ + 1 : 3 * NZ + 1], refs[3 * NZ + 1 : 4 * NZ + 1]
    left_ref, right_ref, prod_ref, part_ref = refs[4 * NZ + 1 :]
    mean, inv_std, gain, shift = (vec_ref[i : i + 1] for i in range(4))
    for k in range(NZ):
        z = jnp.bitwise_and(place_ref[0] + k, NZ - 1)
        left_ref[k * BLK : (k + 1) * BLK, :BLK] = pair_ref[z, 0]
        left_ref[k * BLK : (k + 1) * BLK, BLK:] = mixed[k][...]
        normed, grad_z = silu_parts(hidden[k][...], mean, inv_std, gain, shift, pair_ref[z, 1])
        grad_refs[k][...] = grad_z
        normed_refs[k][...] = normed
        part_ref[0, pl.ds(z, 1), :] = jnp.sum(grad_z, axis=0, keepdims=True)
        part_ref[1, pl.ds(z, 1), :] = jnp.sum(grad_z * normed, axis=0, keepdims=True)
        for i, value in enumerate((grad_z, normed)):
            big = value.astype(BF)
            small = (value - big.astype(F32)).astype(BF)
            right_ref[k * BLK : (k + 1) * BLK, 2 * i * BLK : (2 * i + 1) * BLK] = big
            right_ref[k * BLK : (k + 1) * BLK, (2 * i + 1) * BLK : (2 * i + 2) * BLK] = small
    right_ref[:, 4 * BLK :] = jnp.ones((NZ * BLK, HALF), BF)
    sums = [jnp.sum(part_ref[i], axis=0, keepdims=True) for i in range(2)]
    prod_ref[...] = lax.dot_general(
        left_ref[...], right_ref[...], (((0,), (0,)), ((), ())), preferred_element_type=F32
    )
    mine = prod_ref[pl.ds(pl.multiple_of(place_ref[0] * ROWS, ROWS), ROWS), :]
    with_z = mine[:, :BLK] + mine[:, BLK : 2 * BLK]
    with_n = mine[:, 2 * BLK : 3 * BLK] + mine[:, 3 * BLK : 4 * BLK]
    count = mine[:, 4 * BLK :]
    count = jnp.concatenate([count, count], axis=1)
    for i in range(GROUP):
        part = slice(2 * i, 2 * i + 2)
        payload_ref[i] = jnp.concatenate(
            [*sums, with_z[part], with_n[part], count[part]], axis=0
        )


def backward_kernel(core, half, place_ref, grad, lower, outs, picked_ref, weight_ref, list_ref):
    lane = iota_bf((BLK, BLK), 1)
    tall = BLK if half is None else HALF
    sub = lax.broadcasted_iota(jnp.int32, (tall, BLK), 0) + HALF * (half or 0)
    sub = sub.astype(F32).astype(BF)
    one = jnp.ones((), BF)
    read_lists(lower, list_ref)
    for y in range(NY):
        lists = []
        for k in range(NZ):
            z = jnp.bitwise_and(place_ref[0] + k, NZ - 1)
            lists.append([list_ref[y, pl.ds(field * NZ + z, 1), :] for field in range(4)])
        cols = jnp.concatenate([row[2] for row in lists], axis=0).T
        for k in range(NZ):
            gather = one_hot(lane, cols[:, k : k + 1].astype(BF), one)
            picked = jnp.dot(gather, grad[k], preferred_element_type=F32)
            picked_ref[k * BLK : (k + 1) * BLK] = picked.astype(BF)
            weight_ref[:, k * BLK : (k + 1) * BLK] = one_hot(
                sub, lists[k][0].astype(BF), lists[k][3].astype(BF)
            )
        high = jnp.concatenate([row[1] for row in lists], axis=1)
        step = 1 if half is None else 2
        for x in range(0, NX, step):
            left = [
                weight_ref[...] * jnp.where(high == float(i * NC + core), 1.0, 0.0).astype(BF)
                for i in range(x, x + step)
            ]
            left = left[0] if half is None else jnp.concatenate(left, axis=0)
            out = jnp.dot(left, picked_ref[...], preferred_element_type=F32).astype(BF)
            if half is None:
                outs[0, x * NY + y], outs[1, y * NX + x] = out[:HALF], out[HALF:]
            else:
                for i in range(step):
                    part = out[i * HALF : (i + 1) * HALF]
                    if half:
                        outs[y][x + i] = part
                    else:
                        outs[x + i][y] = part


def totals_kernel(got_ref, vec_ref, out_ref, vec2_ref, term_ref):
    total = got_ref[0]
    for i in range(1, GROUP):
        total = total + got_ref[i]
    root = math.sqrt(GROUP * NZ * BLK)
    scale = vec_ref[1:2] * vec_ref[2:3]
    out_ref[...] = total[:2] * (1.0 / root)
    means = total[:2] * (1.0 / (GROUP * NZ * BLK))
    vec2_ref[...] = jnp.concatenate([scale, means, scale], axis=0)
    term = total[2:4] - total[6:8] * means[0:1] - total[4:6] * means[1:2]
    term_ref[...] = scale * term * (1.0 / root)


def send_kernel(place_ref, vec_ref, self_ref, neigh_ref, lower, *refs):
    grad_z, normed = refs[:NZ], refs[NZ : 2 * NZ]
    send_ref, own_ref, grad_m = refs[2 * NZ : 2 * NZ + 3]
    scale, mean_z, mean_zn = (vec_ref[i : i + 1] for i in range(3))
    for k in range(NZ):
        grad_h = scale * (grad_z[k][...] - mean_z - normed[k][...] * mean_zn)
        grad_h = grad_h.astype(BF)
        grad_m[k] = lax.dot_general(
            grad_h, neigh_ref[...], (((1,), (1,)), ((), ())), preferred_element_type=F32
        ).astype(BF)
        if k == 0:
            own_ref[...] = lax.dot_general(
                grad_h, self_ref[...], (((1,), (1,)), ((), ())), preferred_element_type=F32
            )
    backward_kernel(1, None, place_ref, grad_m, lower, send_ref, *refs[2 * NZ + 3 :])


def keep_kernel(half, place_ref, lower, grad_m, *refs):
    if half:
        other_ref, refs = refs[0], refs[1:]
    backward_kernel(0, half, place_ref, grad_m, lower, refs[:4], *refs[4:])
    if half:
        for y in range(NY):
            refs[y][...] = (refs[y][...].astype(F32) + other_ref[y].astype(F32)).astype(BF)


def swap(value, axis, offset):
    count = {"x": NX, "c": NC, "y": NY, "z": NZ}[axis]
    return lax.ppermute(value, axis, [(i, i ^ offset) for i in range(count)])


def shift(value, step):
    return lax.ppermute(value, "z", [(i, (i + step) % NZ) for i in range(NZ)])


def around(value):
    down, up = [value], [value]
    for _ in range(3):
        down.append(shift(down[-1], 1))
        up.append(shift(up[-1], -1))
    middle = value.shape[0] // 2
    far = [shift(down[3][:middle], 1), shift(up[3][middle:], -1)]
    return up + [jnp.concatenate(far, axis=0)] + down[:0:-1]


def spread_out(value, axis):
    return [value] + [swap(value, axis, k) for k in (1, 2, 3)]


def reduce_in(value, axis):
    got = [swap(value[k], axis, k) for k in (2, 1, 3)]
    return value[0].astype(F32) + sum(part.astype(F32) for part in got)


def exchange(value, axes):
    return lax.all_to_all(value, axes, 0, 0, tiled=False)


def everywhere(value, axes, count):
    return exchange(jnp.broadcast_to(value[None], (count,) + value.shape), axes)


def merge(mean, spread, rows):
    total = jnp.mean(mean, axis=0)
    moved = jnp.sum((mean - total) ** 2, axis=0)
    return total, jnp.sum(spread, axis=0) + rows * moved


def silu_parts(hidden, mean, inv_std, gain, shift, upstream):
    normed = (hidden - mean) * inv_std
    scaled = gain * normed + shift
    sigmoid = jax.nn.sigmoid(scaled)
    grad_z = upstream.astype(F32) * sigmoid * (1.0 + scaled * (1.0 - sigmoid))
    return normed, grad_z


def body(
    features,
    weight_self,
    weight_neigh,
    norm_gain,
    norm_shift,
    upstream,
    source_index,
    target_index,
    edge_weight,
    edge_count,
):
    node_total = BLK * NX * NC * NY * NZ
    root = math.sqrt(node_total)
    place = lax.axis_index("y").astype(jnp.int32)
    place_z = lax.axis_index("z").astype(jnp.int32).reshape(1)
    own = lax.axis_index("x") * NC + lax.axis_index("c")

    pair = jnp.stack([features, upstream])
    turns = [jnp.bitwise_xor(place, k) for k in range(NY)]
    near, pair, turns, place_z, own = lax.optimization_barrier(
        (features, pair, turns, place_z, own)
    )

    source = source_index[0, 0]
    counts = edge_count[0, 0]
    slot = lax.broadcasted_iota(jnp.int32, source.shape, 1)
    weight = jnp.where(slot < counts[:, None], edge_weight[0, 0], jnp.zeros((), BF))
    edges = jnp.stack(
        [
            (source % BLK).astype(F32).astype(BF),
            jnp.bitwise_xor(source // BLK, own).astype(F32).astype(BF),
            target_index[0, 0].astype(F32).astype(BF),
            weight,
        ]
    )
    edges = edges.reshape(4, NY, NZ, BLK).swapaxes(0, 1).reshape(NY, 4 * NZ, BLK)


    pair_all = lax.all_gather(pair, "z", axis=0, tiled=False)
    upper = jnp.stack(spread_out(jnp.stack(spread_out(near[:HALF], "y")), "x"))
    first = spread_out(near[HALF:], "x")
    lower = []
    for k in range(NY):
        lists = lax.dynamic_slice(
            edges, (turns[k], 0, 0), (1, 4 * NZ, BLK), allow_negative_indices=False
        )[0]
        half = jnp.concatenate(first + [lists], axis=0)
        lower.append(swap(half, "y", k) if k else half)
    lower = jnp.stack(lower)
    sources = [upper, swap(upper, "c", 1), lower, swap(lower, "c", 1)]

    block = jax.ShapeDtypeStruct((BLK, BLK), F32)
    carried, arrived = [], []
    for offsets in STEPS:
        if carried:
            carried = [shift(carried[0], 1), shift(carried[1], -1)]
        sources, arrived = lax.optimization_barrier((sources, arrived))
        if offsets is STEPS[1]:
            sources, pair_all = lax.optimization_barrier((sources, pair_all))
        partial = pl.pallas_call(
            functools.partial(forward_kernel, offsets),
            out_shape=(block,) * len(offsets),
            in_specs=[SMEM] + [VMEM] * len(sources),
            out_specs=(VMEM,) * len(offsets),
            scratch_shapes=[pltpu.VMEM((NY * BLK, BLK), BF), LISTS],
            compiler_params=PARAMS,
            cost_estimate=pl.CostEstimate(
                flops=2 * len(offsets) * 10**9, bytes_accessed=5 * 2**20, transcendentals=0
            ),
            name="forward_edges",
        )(place_z, *sources)
        if offsets == (4,):
            carried = [partial[0][:HALF].astype(BF), partial[0][HALF:].astype(BF)]
        elif len(offsets) == 2:
            got = [part.astype(F32) for part in carried]
            if offsets == (3, 5):
                got = [jnp.pad(got[0], ((0, HALF), (0, 0))), jnp.pad(got[1], ((HALF, 0), (0, 0)))]
            arrived = carried
            carried = [(mine + part).astype(BF) for mine, part in zip(partial, got)]
    lower = sources[2]
    mixed = (partial[0] + carried[0].astype(F32) + carried[1].astype(F32)).astype(BF)
    mixed_all = around(mixed)

    blocks = (jax.ShapeDtypeStruct((BLK, BLK), F32),) * NZ
    stats, *hidden_all = pl.pallas_call(
        stats_kernel,
        out_shape=(jax.ShapeDtypeStruct((2, BLK), F32), *blocks),
        in_specs=[SMEM] + [VMEM] * (3 + NZ),
        out_specs=(VMEM,) * (1 + NZ),
        scratch_shapes=[pltpu.VMEM((2, NZ, BLK), F32)],
        compiler_params=PARAMS,
        cost_estimate=pl.CostEstimate(
            flops=10**9, bytes_accessed=5 * 2**20, transcendentals=0
        ),
        name="group_stats",
    )(place_z, weight_self, weight_neigh, pair_all, *mixed_all)
    got = everywhere(stats, ("x", "c", "y"), GROUP)
    col_mean, spread = merge(got[:, 0], got[:, 1], BLK * NZ)
    inv_std = lax.rsqrt(spread / node_total + EPSILON)

    vectors = jnp.stack([col_mean, inv_std, norm_gain, norm_shift])
    payload, *grads = pl.pallas_call(
        group_kernel,
        out_shape=(jax.ShapeDtypeStruct((GROUP, 8, BLK), F32), *blocks, *blocks),
        in_specs=[SMEM] + [VMEM] * (2 + 2 * NZ),
        out_specs=(VMEM,) * (1 + 2 * NZ),
        scratch_shapes=[
            pltpu.VMEM((NZ * BLK, 2 * BLK), BF),
            pltpu.VMEM((NZ * BLK, 4 * BLK + HALF), BF),
            pltpu.VMEM((2 * BLK, 4 * BLK + HALF), F32),
            pltpu.VMEM((2, NZ, BLK), F32),
        ],
        compiler_params=pltpu.CompilerParams(vmem_limit_bytes=20 * 2**20),
        cost_estimate=pl.CostEstimate(
            flops=5 * 10**9, bytes_accessed=8 * 2**20, transcendentals=0
        ),
        name="group_terms",
    )(place_z, vectors, pair_all, *mixed_all, *hidden_all)
    sums, vectors, term = pl.pallas_call(
        totals_kernel,
        out_shape=(
            jax.ShapeDtypeStruct((2, BLK), F32),
            jax.ShapeDtypeStruct((4, BLK), F32),
            jax.ShapeDtypeStruct((2, BLK), F32),
        ),
        in_specs=[VMEM, VMEM],
        out_specs=(VMEM,) * 3,
        compiler_params=PARAMS,
        name="totals",
    )(exchange(payload, ("x", "c", "y")), vectors)
    grad_shift, grad_gain = sums[0], sums[1]

    scratch = [
        pltpu.VMEM((NZ * BLK, BLK), BF),
        pltpu.VMEM((BLK, NZ * BLK), BF),
        LISTS,
    ]
    cost = pl.CostEstimate(flops=8 * 10**9, bytes_accessed=6 * 2**20, transcendentals=0)
    send, own_term, grad_m = pl.pallas_call(
        send_kernel,
        out_shape=(
            jax.ShapeDtypeStruct((2, NX * NY, HALF, BLK), BF),
            jax.ShapeDtypeStruct((BLK, BLK), F32),
            jax.ShapeDtypeStruct((NZ, BLK, BLK), BF),
        ),
        in_specs=[SMEM] + [VMEM] * (4 + 2 * NZ),
        out_specs=(VMEM,) * 3,
        scratch_shapes=scratch,
        compiler_params=PARAMS,
        cost_estimate=cost,
        name="backward_send",
    )(place_z, vectors, weight_self, weight_neigh, lower, *grads)
    other = swap(send, "c", 1).reshape(2, 4, 4, HALF, BLK)
    scratch[1] = pltpu.VMEM((HALF, NZ * BLK), BF)
    both = []
    for half in range(2):
        if half:
            grad_m, both = lax.optimization_barrier((grad_m, both))
        keep = pl.pallas_call(
            functools.partial(keep_kernel, half),
            out_shape=(jax.ShapeDtypeStruct((4, HALF, BLK), BF),) * 4,
            in_specs=[SMEM] + [VMEM] * (2 + half),
            out_specs=(VMEM,) * 4,
            scratch_shapes=scratch,
            compiler_params=PARAMS,
            cost_estimate=cost,
            name="backward_keep",
        )(place_z, lower, grad_m, *([other[1]] if half else []))
        if half:
            both.append(list(keep))
        else:
            both.append(
                [(keep[k].astype(F32) + other[0, k].astype(F32)).astype(BF) for k in range(4)]
            )
        if not half:
            both[0], term = lax.optimization_barrier((both[0], term))
            upper = reduce_in(both[0], "x").astype(BF)
            whole = everywhere(term, ("z", "x", "c", "y"), NZ * GROUP)
    whole = [part.reshape(BLK, BLK) for part in jnp.split(whole, 2)]
    both[1], upper = lax.optimization_barrier((both[1], upper))
    upper = reduce_in(upper, "y")
    lower, whole = lax.optimization_barrier((reduce_in(both[1], "y").astype(BF), whole))
    lower = reduce_in(lower, "x")
    back = jnp.concatenate([upper, lower], axis=0)
    grad_x = (own_term + back).astype(BF)

    return (grad_x, whole[0], whole[1], grad_gain, grad_shift)


def solution(mesh):
    grid = Mesh(mesh.devices.reshape(NX, NC, NY, NZ), ALL)
    row, col = ("x", "c"), ("y", "z")
    placed = (
        P(ALL, None),
        P(),
        P(),
        P(),
        P(),
        P(ALL, None),
        P(row, col, None, None),
        P(row, col, None, None),
        P(row, col, None, None),
        P(row, col, None),
    )
    return jax.shard_map(
        body,
        mesh=grid,
        in_specs=placed,
        out_specs=(P(ALL, None), P(), P(), P(), P()),
        check_vma=False,
    )
```

```python
import functools
import math

import jax
import jax.numpy as jnp
from jax import lax
from jax.experimental import pallas as pl
from jax.experimental.pallas import tpu as pltpu
from jax.sharding import Mesh
from jax.sharding import PartitionSpec as P

EPSILON = 1e-05
BF = jnp.bfloat16
F32 = jnp.float32
NX, NC, NY, NZ = 4, 2, 4, 8
ALL = ("x", "c", "y", "z")
BLK = 256
HALF = 128
GROUP = NX * NC * NY
ROWS = 2 * BLK // NZ
VMEM = pl.BlockSpec(memory_space=pltpu.VMEM)
SMEM = pl.BlockSpec(memory_space=pltpu.SMEM)
PARAMS = pltpu.CompilerParams(vmem_limit_bytes=12 * 2**20)
LISTS = pltpu.VMEM((NY, 4 * NZ, BLK), F32)
STEPS = ((4,), (3, 5), (2, 6), (1, 7), (0,))


def iota_bf(shape, dim):
    return lax.broadcasted_iota(jnp.int32, shape, dim).astype(F32).astype(BF)


def one_hot(iota, index, value):
    return jnp.where(iota == index, value, jnp.zeros((), BF))


def read_lists(lower, list_ref):
    for y in range(NY):
        list_ref[y] = lower[y, NX * HALF :].astype(F32)


def forward_kernel(offsets, place_ref, *refs):
    upper, lower = refs[:2], refs[2:4]
    outs, (picked_ref, list_ref) = refs[4:-2], refs[-2:]
    lane = iota_bf((BLK, BLK), 1)
    sub = iota_bf((BLK, BLK), 0)
    one = jnp.ones((), BF)
    read_lists(lower[0], list_ref)
    for offset, out_ref in zip(offsets, outs):
        z = jnp.bitwise_and(place_ref[0] + offset, NZ - 1)
        scatter = []
        for y in range(NY):
            low, high, target, weight = (
                list_ref[y, pl.ds(field * NZ + z, 1), :] for field in range(4)
            )
            cols = jnp.concatenate([low, high] * 4, axis=0).T
            low = one_hot(lane, cols[:, 0:1].astype(BF), one)
            high = cols[:, 1:2]
            select, rows = [], []
            for x in range(NX):
                for c in range(NC):
                    mask = jnp.where(high == float(x * NC + c), 1.0, 0.0).astype(BF)
                    select.append(low * mask)
                    rows += [upper[c][x, y], lower[c][y, x * HALF : (x + 1) * HALF]]
            picked = jnp.dot(
                jnp.concatenate(select, axis=1),
                jnp.concatenate(rows, axis=0),
                preferred_element_type=F32,
            )
            picked_ref[y * BLK : (y + 1) * BLK] = picked.astype(BF)
            scatter.append(one_hot(sub, target.astype(BF), weight.astype(BF)))
        out = jnp.dot(
            jnp.concatenate(scatter, axis=1), picked_ref[...], preferred_element_type=F32
        )
        out_ref[...] = out


def stats_kernel(place_ref, self_ref, neigh_ref, pair_ref, *refs):
    mixed, stats_ref, hidden_refs, part_ref = refs[:NZ], refs[NZ], refs[NZ + 1 : -1], refs[-1]
    for k in range(NZ):
        z = jnp.bitwise_and(place_ref[0] + k, NZ - 1)
        hidden = jnp.dot(pair_ref[z, 0], self_ref[...], preferred_element_type=F32)
        hidden += jnp.dot(mixed[k][...], neigh_ref[...], preferred_element_type=F32)
        hidden_refs[k][...] = hidden
        mean = jnp.sum(hidden, axis=0, keepdims=True) * (1.0 / BLK)
        part_ref[0, pl.ds(z, 1), :] = mean
        part_ref[1, pl.ds(z, 1), :] = jnp.sum((hidden - mean) ** 2, axis=0, keepdims=True)
    means, spreads = part_ref[0], part_ref[1]
    parts = [(means[z : z + 1], spreads[z : z + 1]) for z in range(NZ)]
    rows = BLK
    while len(parts) > 1:
        parts = [
            ((m0 + m1) * 0.5, s0 + s1 + (0.5 * rows) * (m0 - m1) ** 2)
            for (m0, s0), (m1, s1) in zip(parts[::2], parts[1::2])
        ]
        rows *= 2
    stats_ref[...] = jnp.concatenate(parts[0], axis=0)


def group_kernel(place_ref, vec_ref, pair_ref, *refs):
    mixed, hidden, payload_ref = refs[:NZ], refs[NZ : 2 * NZ], refs[2 * NZ]
    grad_refs, normed_refs = refs[2 * NZ + 1 : 3 * NZ + 1], refs[3 * NZ + 1 : 4 * NZ + 1]
    left_ref, right_ref, prod_ref, part_ref = refs[4 * NZ + 1 :]
    mean, inv_std, gain, shift = (vec_ref[i : i + 1] for i in range(4))
    for k in range(NZ):
        z = jnp.bitwise_and(place_ref[0] + k, NZ - 1)
        left_ref[k * BLK : (k + 1) * BLK, :BLK] = pair_ref[z, 0]
        left_ref[k * BLK : (k + 1) * BLK, BLK:] = mixed[k][...]
        normed, grad_z = silu_parts(hidden[k][...], mean, inv_std, gain, shift, pair_ref[z, 1])
        grad_refs[k][...] = grad_z
        normed_refs[k][...] = normed
        part_ref[0, pl.ds(z, 1), :] = jnp.sum(grad_z, axis=0, keepdims=True)
        part_ref[1, pl.ds(z, 1), :] = jnp.sum(grad_z * normed, axis=0, keepdims=True)
        for i, value in enumerate((grad_z, normed)):
            big = value.astype(BF)
            small = (value - big.astype(F32)).astype(BF)
            right_ref[k * BLK : (k + 1) * BLK, 2 * i * BLK : (2 * i + 1) * BLK] = big
            right_ref[k * BLK : (k + 1) * BLK, (2 * i + 1) * BLK : (2 * i + 2) * BLK] = small
    right_ref[:, 4 * BLK :] = jnp.ones((NZ * BLK, HALF), BF)
    sums = [jnp.sum(part_ref[i], axis=0, keepdims=True) for i in range(2)]
    prod_ref[...] = lax.dot_general(
        left_ref[...], right_ref[...], (((0,), (0,)), ((), ())), preferred_element_type=F32
    )
    mine = prod_ref[pl.ds(pl.multiple_of(place_ref[0] * ROWS, ROWS), ROWS), :]
    with_z = mine[:, :BLK] + mine[:, BLK : 2 * BLK]
    with_n = mine[:, 2 * BLK : 3 * BLK] + mine[:, 3 * BLK : 4 * BLK]
    count = mine[:, 4 * BLK :]
    count = jnp.concatenate([count, count], axis=1)
    for i in range(GROUP):
        part = slice(2 * i, 2 * i + 2)
        payload_ref[i] = jnp.concatenate(
            [*sums, with_z[part], with_n[part], count[part]], axis=0
        )


def backward_kernel(core, half, place_ref, grad, lower, outs, picked_ref, weight_ref, list_ref):
    lane = iota_bf((BLK, BLK), 1)
    tall = BLK if half is None else HALF
    sub = lax.broadcasted_iota(jnp.int32, (tall, BLK), 0) + HALF * (half or 0)
    sub = sub.astype(F32).astype(BF)
    one = jnp.ones((), BF)
    read_lists(lower, list_ref)
    for y in range(NY):
        lists = []
        for k in range(NZ):
            z = jnp.bitwise_and(place_ref[0] + k, NZ - 1)
            lists.append([list_ref[y, pl.ds(field * NZ + z, 1), :] for field in range(4)])
        cols = jnp.concatenate([row[2] for row in lists], axis=0).T
        for k in range(NZ):
            gather = one_hot(lane, cols[:, k : k + 1].astype(BF), one)
            picked = jnp.dot(gather, grad[k], preferred_element_type=F32)
            picked_ref[k * BLK : (k + 1) * BLK] = picked.astype(BF)
            weight_ref[:, k * BLK : (k + 1) * BLK] = one_hot(
                sub, lists[k][0].astype(BF), lists[k][3].astype(BF)
            )
        high = jnp.concatenate([row[1] for row in lists], axis=1)
        step = 1 if half is None else 2
        for x in range(0, NX, step):
            left = [
                weight_ref[...] * jnp.where(high == float(i * NC + core), 1.0, 0.0).astype(BF)
                for i in range(x, x + step)
            ]
            left = left[0] if half is None else jnp.concatenate(left, axis=0)
            out = jnp.dot(left, picked_ref[...], preferred_element_type=F32).astype(BF)
            if half is None:
                outs[0, x * NY + y], outs[1, y * NX + x] = out[:HALF], out[HALF:]
            else:
                for i in range(step):
                    part = out[i * HALF : (i + 1) * HALF]
                    if half:
                        outs[y][x + i] = part
                    else:
                        outs[x + i][y] = part


def totals_kernel(got_ref, vec_ref, out_ref, vec2_ref, term_ref):
    total = got_ref[0]
    for i in range(1, GROUP):
        total = total + got_ref[i]
    root = math.sqrt(GROUP * NZ * BLK)
    scale = vec_ref[1:2] * vec_ref[2:3]
    out_ref[...] = total[:2] * (1.0 / root)
    means = total[:2] * (1.0 / (GROUP * NZ * BLK))
    vec2_ref[...] = jnp.concatenate([scale, means, scale], axis=0)
    term = total[2:4] - total[6:8] * means[0:1] - total[4:6] * means[1:2]
    term_ref[...] = scale * term * (1.0 / root)


def send_kernel(place_ref, vec_ref, self_ref, neigh_ref, lower, *refs):
    grad_z, normed = refs[:NZ], refs[NZ : 2 * NZ]
    send_ref, own_ref, grad_m = refs[2 * NZ : 2 * NZ + 3]
    scale, mean_z, mean_zn = (vec_ref[i : i + 1] for i in range(3))
    for k in range(NZ):
        grad_h = scale * (grad_z[k][...] - mean_z - normed[k][...] * mean_zn)
        grad_h = grad_h.astype(BF)
        grad_m[k] = lax.dot_general(
            grad_h, neigh_ref[...], (((1,), (1,)), ((), ())), preferred_element_type=F32
        ).astype(BF)
        if k == 0:
            own_ref[...] = lax.dot_general(
                grad_h, self_ref[...], (((1,), (1,)), ((), ())), preferred_element_type=F32
            )
    backward_kernel(1, None, place_ref, grad_m, lower, send_ref, *refs[2 * NZ + 3 :])


def keep_kernel(half, place_ref, lower, grad_m, *refs):
    if half:
        other_ref, refs = refs[0], refs[1:]
    backward_kernel(0, half, place_ref, grad_m, lower, refs[:4], *refs[4:])
    if half:
        for y in range(NY):
            refs[y][...] = (refs[y][...].astype(F32) + other_ref[y].astype(F32)).astype(BF)


def swap(value, axis, offset):
    count = {"x": NX, "c": NC, "y": NY, "z": NZ}[axis]
    return lax.ppermute(value, axis, [(i, i ^ offset) for i in range(count)])


def shift(value, step):
    return lax.ppermute(value, "z", [(i, (i + step) % NZ) for i in range(NZ)])


def around(value):
    down, up = [value], [value]
    for _ in range(3):
        down.append(shift(down[-1], 1))
        up.append(shift(up[-1], -1))
    middle = value.shape[0] // 2
    far = [shift(down[3][:middle], 1), shift(up[3][middle:], -1)]
    return up + [jnp.concatenate(far, axis=0)] + down[:0:-1]


def spread_out(value, axis):
    return [value] + [swap(value, axis, k) for k in (1, 2, 3)]


def reduce_in(value, axis, beside=None):
    got = [swap(value[k], axis, k) for k in (2, 1, 3)]
    if beside is not None:
        got, beside = lax.optimization_barrier((got, beside))
        return value[0].astype(F32) + sum(part.astype(F32) for part in got), beside
    return value[0].astype(F32) + sum(part.astype(F32) for part in got)


def exchange(value, axes):
    return lax.all_to_all(value, axes, 0, 0, tiled=False)


def everywhere(value, axes, count):
    return exchange(jnp.broadcast_to(value[None], (count,) + value.shape), axes)


def merge(mean, spread, rows):
    total = jnp.mean(mean, axis=0)
    moved = jnp.sum((mean - total) ** 2, axis=0)
    return total, jnp.sum(spread, axis=0) + rows * moved


def silu_parts(hidden, mean, inv_std, gain, shift, upstream):
    normed = (hidden - mean) * inv_std
    scaled = gain * normed + shift
    sigmoid = jax.nn.sigmoid(scaled)
    grad_z = upstream.astype(F32) * sigmoid * (1.0 + scaled * (1.0 - sigmoid))
    return normed, grad_z


def body(
    features,
    weight_self,
    weight_neigh,
    norm_gain,
    norm_shift,
    upstream,
    source_index,
    target_index,
    edge_weight,
    edge_count,
):
    node_total = BLK * NX * NC * NY * NZ
    root = math.sqrt(node_total)
    place = lax.axis_index("y").astype(jnp.int32)
    place_z = lax.axis_index("z").astype(jnp.int32).reshape(1)
    own = lax.axis_index("x") * NC + lax.axis_index("c")

    pair = jnp.stack([features, upstream])
    turns = [jnp.bitwise_xor(place, k) for k in range(NY)]
    near, pair, turns, place_z, own = lax.optimization_barrier(
        (features, pair, turns, place_z, own)
    )

    source = source_index[0, 0]
    counts = edge_count[0, 0]
    slot = lax.broadcasted_iota(jnp.int32, source.shape, 1)
    weight = jnp.where(slot < counts[:, None], edge_weight[0, 0], jnp.zeros((), BF))
    edges = jnp.stack(
        [
            (source % BLK).astype(F32).astype(BF),
            jnp.bitwise_xor(source // BLK, own).astype(F32).astype(BF),
            target_index[0, 0].astype(F32).astype(BF),
            weight,
        ]
    )
    edges = edges.reshape(4, NY, NZ, BLK).swapaxes(0, 1).reshape(NY, 4 * NZ, BLK)


    pair_all = lax.all_gather(pair, "z", axis=0, tiled=False)
    upper = jnp.stack(spread_out(jnp.stack(spread_out(near[:HALF], "y")), "x"))
    first = spread_out(near[HALF:], "x")
    lower = []
    for k in range(NY):
        lists = lax.dynamic_slice(
            edges, (turns[k], 0, 0), (1, 4 * NZ, BLK), allow_negative_indices=False
        )[0]
        half = jnp.concatenate(first + [lists], axis=0)
        lower.append(swap(half, "y", k) if k else half)
    lower = jnp.stack(lower)
    sources = [upper, swap(upper, "c", 1), lower, swap(lower, "c", 1)]

    block = jax.ShapeDtypeStruct((BLK, BLK), F32)
    carried, arrived = [], []
    for offsets in STEPS:
        if carried:
            carried = [shift(carried[0], 1), shift(carried[1], -1)]
        sources, arrived = lax.optimization_barrier((sources, arrived))
        if offsets is STEPS[1]:
            sources, pair_all = lax.optimization_barrier((sources, pair_all))
        partial = pl.pallas_call(
            functools.partial(forward_kernel, offsets),
            out_shape=(block,) * len(offsets),
            in_specs=[SMEM] + [VMEM] * len(sources),
            out_specs=(VMEM,) * len(offsets),
            scratch_shapes=[pltpu.VMEM((NY * BLK, BLK), BF), LISTS],
            compiler_params=PARAMS,
            cost_estimate=pl.CostEstimate(
                flops=2 * len(offsets) * 10**9, bytes_accessed=5 * 2**20, transcendentals=0
            ),
            name="forward_edges",
        )(place_z, *sources)
        if offsets == (4,):
            carried = [partial[0][:HALF].astype(BF), partial[0][HALF:].astype(BF)]
        elif len(offsets) == 2:
            got = [part.astype(F32) for part in carried]
            if offsets == (3, 5):
                got = [jnp.pad(got[0], ((0, HALF), (0, 0))), jnp.pad(got[1], ((HALF, 0), (0, 0)))]
            arrived = carried
            carried = [(mine + part).astype(BF) for mine, part in zip(partial, got)]
    lower = sources[2]
    mixed = (partial[0] + carried[0].astype(F32) + carried[1].astype(F32)).astype(BF)
    mixed_all = around(mixed)

    blocks = (jax.ShapeDtypeStruct((BLK, BLK), F32),) * NZ
    stats, *hidden_all = pl.pallas_call(
        stats_kernel,
        out_shape=(jax.ShapeDtypeStruct((2, BLK), F32), *blocks),
        in_specs=[SMEM] + [VMEM] * (3 + NZ),
        out_specs=(VMEM,) * (1 + NZ),
        scratch_shapes=[pltpu.VMEM((2, NZ, BLK), F32)],
        compiler_params=PARAMS,
        cost_estimate=pl.CostEstimate(
            flops=10**9, bytes_accessed=5 * 2**20, transcendentals=0
        ),
        name="group_stats",
    )(place_z, weight_self, weight_neigh, pair_all, *mixed_all)
    got = everywhere(stats, ("x", "c", "y"), GROUP)
    col_mean, spread = merge(got[:, 0], got[:, 1], BLK * NZ)
    inv_std = lax.rsqrt(spread / node_total + EPSILON)

    vectors = jnp.stack([col_mean, inv_std, norm_gain, norm_shift])
    payload, *grads = pl.pallas_call(
        group_kernel,
        out_shape=(jax.ShapeDtypeStruct((GROUP, 8, BLK), F32), *blocks, *blocks),
        in_specs=[SMEM] + [VMEM] * (2 + 2 * NZ),
        out_specs=(VMEM,) * (1 + 2 * NZ),
        scratch_shapes=[
            pltpu.VMEM((NZ * BLK, 2 * BLK), BF),
            pltpu.VMEM((NZ * BLK, 4 * BLK + HALF), BF),
            pltpu.VMEM((2 * BLK, 4 * BLK + HALF), F32),
            pltpu.VMEM((2, NZ, BLK), F32),
        ],
        compiler_params=pltpu.CompilerParams(vmem_limit_bytes=20 * 2**20),
        cost_estimate=pl.CostEstimate(
            flops=5 * 10**9, bytes_accessed=8 * 2**20, transcendentals=0
        ),
        name="group_terms",
    )(place_z, vectors, pair_all, *mixed_all, *hidden_all)
    sums, vectors, term = pl.pallas_call(
        totals_kernel,
        out_shape=(
            jax.ShapeDtypeStruct((2, BLK), F32),
            jax.ShapeDtypeStruct((4, BLK), F32),
            jax.ShapeDtypeStruct((2, BLK), F32),
        ),
        in_specs=[VMEM, VMEM],
        out_specs=(VMEM,) * 3,
        compiler_params=PARAMS,
        name="totals",
    )(exchange(payload, ("x", "c", "y")), vectors)
    grad_shift, grad_gain = sums[0], sums[1]

    scratch = [
        pltpu.VMEM((NZ * BLK, BLK), BF),
        pltpu.VMEM((BLK, NZ * BLK), BF),
        LISTS,
    ]
    cost = pl.CostEstimate(flops=8 * 10**9, bytes_accessed=6 * 2**20, transcendentals=0)
    send, own_term, grad_m = pl.pallas_call(
        send_kernel,
        out_shape=(
            jax.ShapeDtypeStruct((2, NX * NY, HALF, BLK), BF),
            jax.ShapeDtypeStruct((BLK, BLK), F32),
            jax.ShapeDtypeStruct((NZ, BLK, BLK), BF),
        ),
        in_specs=[SMEM] + [VMEM] * (4 + 2 * NZ),
        out_specs=(VMEM,) * 3,
        scratch_shapes=scratch,
        compiler_params=PARAMS,
        cost_estimate=cost,
        name="backward_send",
    )(place_z, vectors, weight_self, weight_neigh, lower, *grads)
    other = swap(send, "c", 1).reshape(2, 4, 4, HALF, BLK)
    scratch[1] = pltpu.VMEM((HALF, NZ * BLK), BF)
    both = []
    for half in range(2):
        if half:
            grad_m, both = lax.optimization_barrier((grad_m, both))
        keep = pl.pallas_call(
            functools.partial(keep_kernel, half),
            out_shape=(jax.ShapeDtypeStruct((4, HALF, BLK), BF),) * 4,
            in_specs=[SMEM] + [VMEM] * (2 + half),
            out_specs=(VMEM,) * 4,
            scratch_shapes=scratch,
            compiler_params=PARAMS,
            cost_estimate=cost,
            name="backward_keep",
        )(place_z, lower, grad_m, *([other[1]] if half else []))
        if half:
            both.append(list(keep))
        else:
            both.append(
                [(keep[k].astype(F32) + other[0, k].astype(F32)).astype(BF) for k in range(4)]
            )
        if not half:
            both[0], term = lax.optimization_barrier((both[0], term))
            upper = reduce_in(both[0], "x").astype(BF)
            whole = everywhere(term, ("z", "x", "c", "y"), NZ * GROUP)
    whole = [part.reshape(BLK, BLK) for part in jnp.split(whole, 2)]
    both[1], upper = lax.optimization_barrier((both[1], upper))
    upper = reduce_in(upper, "y")
    lower, whole = reduce_in(both[1], "y", whole)
    lower = reduce_in(lower.astype(BF), "x")
    back = jnp.concatenate([upper, lower], axis=0)
    grad_x = (own_term + back).astype(BF)

    return (grad_x, whole[0], whole[1], grad_gain, grad_shift)


def solution(mesh):
    grid = Mesh(mesh.devices.reshape(NX, NC, NY, NZ), ALL)
    row, col = ("x", "c"), ("y", "z")
    placed = (
        P(ALL, None),
        P(),
        P(),
        P(),
        P(),
        P(ALL, None),
        P(row, col, None, None),
        P(row, col, None, None),
        P(row, col, None, None),
        P(row, col, None),
    )
    return jax.shard_map(
        body,
        mesh=grid,
        in_specs=placed,
        out_specs=(P(ALL, None), P(), P(), P(), P()),
        check_vma=False,
    )
```

```python
import functools
import math

import jax
import jax.numpy as jnp
from jax import lax
from jax.experimental import pallas as pl
from jax.experimental.pallas import tpu as pltpu
from jax.sharding import Mesh
from jax.sharding import PartitionSpec as P

EPSILON = 1e-05
BF = jnp.bfloat16
F32 = jnp.float32
NX, NC, NY, NZ = 4, 2, 4, 8
ALL = ("x", "c", "y", "z")
BLK = 256
HALF = 128
GROUP = NX * NC * NY
ROWS = 2 * BLK // NZ
VMEM = pl.BlockSpec(memory_space=pltpu.VMEM)
SMEM = pl.BlockSpec(memory_space=pltpu.SMEM)
PARAMS = pltpu.CompilerParams(vmem_limit_bytes=12 * 2**20)
LISTS = pltpu.VMEM((NY, 4 * NZ, BLK), F32)
STEPS = ((4,), (3, 5), (2, 6), (1, 7), (0,))


def iota_bf(shape, dim):
    return lax.broadcasted_iota(jnp.int32, shape, dim).astype(F32).astype(BF)


def one_hot(iota, index, value):
    return jnp.where(iota == index, value, jnp.zeros((), BF))


def read_lists(lower, list_ref):
    for y in range(NY):
        list_ref[y] = lower[y, NX * HALF :].astype(F32)


def forward_kernel(offsets, place_ref, *refs):
    upper, lower = refs[:2], refs[2:4]
    outs, (picked_ref, list_ref) = refs[4:-2], refs[-2:]
    lane = iota_bf((BLK, BLK), 1)
    sub = iota_bf((BLK, BLK), 0)
    one = jnp.ones((), BF)
    read_lists(lower[0], list_ref)
    for offset, out_ref in zip(offsets, outs):
        z = jnp.bitwise_and(place_ref[0] + offset, NZ - 1)
        scatter = []
        for y in range(NY):
            low, high, target, weight = (
                list_ref[y, pl.ds(field * NZ + z, 1), :] for field in range(4)
            )
            cols = jnp.concatenate([low, high] * 4, axis=0).T
            low = one_hot(lane, cols[:, 0:1].astype(BF), one)
            high = cols[:, 1:2]
            select, rows = [], []
            for x in range(NX):
                for c in range(NC):
                    mask = jnp.where(high == float(x * NC + c), 1.0, 0.0).astype(BF)
                    select.append(low * mask)
                    rows += [upper[c][x, y], lower[c][y, x * HALF : (x + 1) * HALF]]
            picked = jnp.dot(
                jnp.concatenate(select, axis=1),
                jnp.concatenate(rows, axis=0),
                preferred_element_type=F32,
            )
            picked_ref[y * BLK : (y + 1) * BLK] = picked.astype(BF)
            scatter.append(one_hot(sub, target.astype(BF), weight.astype(BF)))
        out = jnp.dot(
            jnp.concatenate(scatter, axis=1), picked_ref[...], preferred_element_type=F32
        )
        out_ref[...] = out


def stats_kernel(place_ref, self_ref, neigh_ref, pair_ref, *refs):
    mixed, stats_ref, hidden_refs, part_ref = refs[:NZ], refs[NZ], refs[NZ + 1 : -1], refs[-1]
    for k in range(NZ):
        z = jnp.bitwise_and(place_ref[0] + k, NZ - 1)
        hidden = jnp.dot(pair_ref[z, 0], self_ref[...], preferred_element_type=F32)
        hidden += jnp.dot(mixed[k][...], neigh_ref[...], preferred_element_type=F32)
        hidden_refs[k][...] = hidden
        mean = jnp.sum(hidden, axis=0, keepdims=True) * (1.0 / BLK)
        part_ref[0, pl.ds(z, 1), :] = mean
        part_ref[1, pl.ds(z, 1), :] = jnp.sum((hidden - mean) ** 2, axis=0, keepdims=True)
    means, spreads = part_ref[0], part_ref[1]
    parts = [(means[z : z + 1], spreads[z : z + 1]) for z in range(NZ)]
    rows = BLK
    while len(parts) > 1:
        parts = [
            ((m0 + m1) * 0.5, s0 + s1 + (0.5 * rows) * (m0 - m1) ** 2)
            for (m0, s0), (m1, s1) in zip(parts[::2], parts[1::2])
        ]
        rows *= 2
    stats_ref[...] = jnp.concatenate(parts[0], axis=0)


def group_kernel(place_ref, vec_ref, pair_ref, *refs):
    mixed, hidden, payload_ref = refs[:NZ], refs[NZ : 2 * NZ], refs[2 * NZ]
    grad_refs, normed_refs = refs[2 * NZ + 1 : 3 * NZ + 1], refs[3 * NZ + 1 : 4 * NZ + 1]
    left_ref, right_ref, prod_ref, part_ref = refs[4 * NZ + 1 :]
    mean, inv_std, gain, shift = (vec_ref[i : i + 1] for i in range(4))
    for k in range(NZ):
        z = jnp.bitwise_and(place_ref[0] + k, NZ - 1)
        left_ref[k * BLK : (k + 1) * BLK, :BLK] = pair_ref[z, 0]
        left_ref[k * BLK : (k + 1) * BLK, BLK:] = mixed[k][...]
        normed, grad_z = silu_parts(hidden[k][...], mean, inv_std, gain, shift, pair_ref[z, 1])
        grad_refs[k][...] = grad_z
        normed_refs[k][...] = normed
        part_ref[0, pl.ds(z, 1), :] = jnp.sum(grad_z, axis=0, keepdims=True)
        part_ref[1, pl.ds(z, 1), :] = jnp.sum(grad_z * normed, axis=0, keepdims=True)
        for i, value in enumerate((grad_z, normed)):
            big = value.astype(BF)
            small = (value - big.astype(F32)).astype(BF)
            right_ref[k * BLK : (k + 1) * BLK, 2 * i * BLK : (2 * i + 1) * BLK] = big
            right_ref[k * BLK : (k + 1) * BLK, (2 * i + 1) * BLK : (2 * i + 2) * BLK] = small
    right_ref[:, 4 * BLK :] = jnp.ones((NZ * BLK, HALF), BF)
    sums = [jnp.sum(part_ref[i], axis=0, keepdims=True) for i in range(2)]
    prod_ref[...] = lax.dot_general(
        left_ref[...], right_ref[...], (((0,), (0,)), ((), ())), preferred_element_type=F32
    )
    mine = prod_ref[pl.ds(pl.multiple_of(place_ref[0] * ROWS, ROWS), ROWS), :]
    with_z = mine[:, :BLK] + mine[:, BLK : 2 * BLK]
    with_n = mine[:, 2 * BLK : 3 * BLK] + mine[:, 3 * BLK : 4 * BLK]
    count = mine[:, 4 * BLK :]
    count = jnp.concatenate([count, count], axis=1)
    for i in range(GROUP):
        part = slice(2 * i, 2 * i + 2)
        payload_ref[i] = jnp.concatenate(
            [*sums, with_z[part], with_n[part], count[part]], axis=0
        )


def backward_kernel(core, half, place_ref, grad, lower, outs, picked_ref, weight_ref, list_ref):
    lane = iota_bf((BLK, BLK), 1)
    tall = BLK if half is None else HALF
    sub = lax.broadcasted_iota(jnp.int32, (tall, BLK), 0) + HALF * (half or 0)
    sub = sub.astype(F32).astype(BF)
    one = jnp.ones((), BF)
    read_lists(lower, list_ref)
    for y in range(NY):
        lists = []
        for k in range(NZ):
            z = jnp.bitwise_and(place_ref[0] + k, NZ - 1)
            lists.append([list_ref[y, pl.ds(field * NZ + z, 1), :] for field in range(4)])
        cols = jnp.concatenate([row[2] for row in lists], axis=0).T
        for k in range(NZ):
            gather = one_hot(lane, cols[:, k : k + 1].astype(BF), one)
            picked = jnp.dot(gather, grad[k], preferred_element_type=F32)
            picked_ref[k * BLK : (k + 1) * BLK] = picked.astype(BF)
            weight_ref[:, k * BLK : (k + 1) * BLK] = one_hot(
                sub, lists[k][0].astype(BF), lists[k][3].astype(BF)
            )
        high = jnp.concatenate([row[1] for row in lists], axis=1)
        step = 1 if half is None else 2
        for x in range(0, NX, step):
            left = [
                weight_ref[...] * jnp.where(high == float(i * NC + core), 1.0, 0.0).astype(BF)
                for i in range(x, x + step)
            ]
            left = left[0] if half is None else jnp.concatenate(left, axis=0)
            out = jnp.dot(left, picked_ref[...], preferred_element_type=F32).astype(BF)
            if half is None:
                outs[0][x, y], outs[1][y, x] = out[:HALF], out[HALF:]
            else:
                for i in range(step):
                    part = out[i * HALF : (i + 1) * HALF]
                    if half:
                        outs[y][x + i] = part
                    else:
                        outs[x + i][y] = part


def totals_kernel(got_ref, vec_ref, out_ref, vec2_ref, term_ref):
    total = got_ref[0]
    for i in range(1, GROUP):
        total = total + got_ref[i]
    root = math.sqrt(GROUP * NZ * BLK)
    scale = vec_ref[1:2] * vec_ref[2:3]
    out_ref[...] = total[:2] * (1.0 / root)
    means = total[:2] * (1.0 / (GROUP * NZ * BLK))
    vec2_ref[...] = jnp.concatenate([scale, means, scale], axis=0)
    term = total[2:4] - total[6:8] * means[0:1] - total[4:6] * means[1:2]
    term_ref[...] = scale * term * (1.0 / root)


def send_kernel(place_ref, vec_ref, self_ref, neigh_ref, lower, *refs):
    grad_z, normed = refs[:NZ], refs[NZ : 2 * NZ]
    upper_ref, lower_ref, own_ref, grad_m = refs[2 * NZ : 2 * NZ + 4]
    scale, mean_z, mean_zn = (vec_ref[i : i + 1] for i in range(3))
    for k in range(NZ):
        grad_h = scale * (grad_z[k][...] - mean_z - normed[k][...] * mean_zn)
        grad_h = grad_h.astype(BF)
        grad_m[k] = lax.dot_general(
            grad_h, neigh_ref[...], (((1,), (1,)), ((), ())), preferred_element_type=F32
        ).astype(BF)
        if k == 0:
            own_ref[...] = lax.dot_general(
                grad_h, self_ref[...], (((1,), (1,)), ((), ())), preferred_element_type=F32
            )
    backward_kernel(1, None, place_ref, grad_m, lower, (upper_ref, lower_ref), *refs[2 * NZ + 4 :])


def keep_kernel(half, place_ref, lower, grad_m, *refs):
    if half:
        other_ref, refs = refs[0], refs[1:]
    backward_kernel(0, half, place_ref, grad_m, lower, refs[:4], *refs[4:])
    if half:
        for y in range(NY):
            refs[y][...] = (refs[y][...].astype(F32) + other_ref[y].astype(F32)).astype(BF)


def swap(value, axis, offset):
    count = {"x": NX, "c": NC, "y": NY, "z": NZ}[axis]
    return lax.ppermute(value, axis, [(i, i ^ offset) for i in range(count)])


def shift(value, step):
    return lax.ppermute(value, "z", [(i, (i + step) % NZ) for i in range(NZ)])


def around(value):
    down, up = [value], [value]
    for _ in range(3):
        down.append(shift(down[-1], 1))
        up.append(shift(up[-1], -1))
    middle = value.shape[0] // 2
    far = [shift(down[3][:middle], 1), shift(up[3][middle:], -1)]
    return up + [jnp.concatenate(far, axis=0)] + down[:0:-1]


def spread_out(value, axis):
    return [value] + [swap(value, axis, k) for k in (1, 2, 3)]


def reduce_in(value, axis, beside=None):
    got = [swap(value[k], axis, k) for k in (2, 1, 3)]
    if beside is not None:
        got, beside = lax.optimization_barrier((got, beside))
        return value[0].astype(F32) + sum(part.astype(F32) for part in got), beside
    return value[0].astype(F32) + sum(part.astype(F32) for part in got)


def exchange(value, axes):
    return lax.all_to_all(value, axes, 0, 0, tiled=False)


def everywhere(value, axes, count):
    return exchange(jnp.broadcast_to(value[None], (count,) + value.shape), axes)


def merge(mean, spread, rows):
    total = jnp.mean(mean, axis=0)
    moved = jnp.sum((mean - total) ** 2, axis=0)
    return total, jnp.sum(spread, axis=0) + rows * moved


def silu_parts(hidden, mean, inv_std, gain, shift, upstream):
    normed = (hidden - mean) * inv_std
    scaled = gain * normed + shift
    sigmoid = jax.nn.sigmoid(scaled)
    grad_z = upstream.astype(F32) * sigmoid * (1.0 + scaled * (1.0 - sigmoid))
    return normed, grad_z


def body(
    features,
    weight_self,
    weight_neigh,
    norm_gain,
    norm_shift,
    upstream,
    source_index,
    target_index,
    edge_weight,
    edge_count,
):
    node_total = BLK * NX * NC * NY * NZ
    root = math.sqrt(node_total)
    place = lax.axis_index("y").astype(jnp.int32)
    place_z = lax.axis_index("z").astype(jnp.int32).reshape(1)
    own = lax.axis_index("x") * NC + lax.axis_index("c")

    pair = jnp.stack([features, upstream])
    turns = [jnp.bitwise_xor(place, k) for k in range(NY)]
    near, pair, turns, place_z, own = lax.optimization_barrier(
        (features, pair, turns, place_z, own)
    )

    source = source_index[0, 0]
    counts = edge_count[0, 0]
    slot = lax.broadcasted_iota(jnp.int32, source.shape, 1)
    weight = jnp.where(slot < counts[:, None], edge_weight[0, 0], jnp.zeros((), BF))
    edges = jnp.stack(
        [
            (source % BLK).astype(F32).astype(BF),
            jnp.bitwise_xor(source // BLK, own).astype(F32).astype(BF),
            target_index[0, 0].astype(F32).astype(BF),
            weight,
        ]
    )
    edges = edges.reshape(4, NY, NZ, BLK).swapaxes(0, 1).reshape(NY, 4 * NZ, BLK)


    pair_all = lax.all_gather(pair, "z", axis=0, tiled=False)
    upper = jnp.stack(spread_out(jnp.stack(spread_out(near[:HALF], "y")), "x"))
    first = spread_out(near[HALF:], "x")
    lower = []
    for k in range(NY):
        lists = lax.dynamic_slice(
            edges, (turns[k], 0, 0), (1, 4 * NZ, BLK), allow_negative_indices=False
        )[0]
        half = jnp.concatenate(first + [lists], axis=0)
        lower.append(swap(half, "y", k) if k else half)
    lower = jnp.stack(lower)
    sources = [upper, swap(upper, "c", 1), lower, swap(lower, "c", 1)]

    block = jax.ShapeDtypeStruct((BLK, BLK), F32)
    carried, arrived = [], []
    for offsets in STEPS:
        if carried:
            carried = [shift(carried[0], 1), shift(carried[1], -1)]
        sources, arrived = lax.optimization_barrier((sources, arrived))
        if offsets is STEPS[1]:
            sources, pair_all = lax.optimization_barrier((sources, pair_all))
        partial = pl.pallas_call(
            functools.partial(forward_kernel, offsets),
            out_shape=(block,) * len(offsets),
            in_specs=[SMEM] + [VMEM] * len(sources),
            out_specs=(VMEM,) * len(offsets),
            scratch_shapes=[pltpu.VMEM((NY * BLK, BLK), BF), LISTS],
            compiler_params=PARAMS,
            cost_estimate=pl.CostEstimate(
                flops=2 * len(offsets) * 10**9, bytes_accessed=5 * 2**20, transcendentals=0
            ),
            name="forward_edges",
        )(place_z, *sources)
        if offsets == (4,):
            carried = [partial[0][:HALF].astype(BF), partial[0][HALF:].astype(BF)]
        elif len(offsets) == 2:
            got = [part.astype(F32) for part in carried]
            if offsets == (3, 5):
                got = [jnp.pad(got[0], ((0, HALF), (0, 0))), jnp.pad(got[1], ((HALF, 0), (0, 0)))]
            arrived = carried
            carried = [(mine + part).astype(BF) for mine, part in zip(partial, got)]
    lower = sources[2]
    mixed = (partial[0] + carried[0].astype(F32) + carried[1].astype(F32)).astype(BF)
    mixed_all = around(mixed)

    blocks = (jax.ShapeDtypeStruct((BLK, BLK), F32),) * NZ
    stats, *hidden_all = pl.pallas_call(
        stats_kernel,
        out_shape=(jax.ShapeDtypeStruct((2, BLK), F32), *blocks),
        in_specs=[SMEM] + [VMEM] * (3 + NZ),
        out_specs=(VMEM,) * (1 + NZ),
        scratch_shapes=[pltpu.VMEM((2, NZ, BLK), F32)],
        compiler_params=PARAMS,
        cost_estimate=pl.CostEstimate(
            flops=10**9, bytes_accessed=5 * 2**20, transcendentals=0
        ),
        name="group_stats",
    )(place_z, weight_self, weight_neigh, pair_all, *mixed_all)
    got = everywhere(stats, ("x", "c", "y"), GROUP)
    col_mean, spread = merge(got[:, 0], got[:, 1], BLK * NZ)
    inv_std = lax.rsqrt(spread / node_total + EPSILON)

    vectors = jnp.stack([col_mean, inv_std, norm_gain, norm_shift])
    payload, *grads = pl.pallas_call(
        group_kernel,
        out_shape=(jax.ShapeDtypeStruct((GROUP, 8, BLK), F32), *blocks, *blocks),
        in_specs=[SMEM] + [VMEM] * (2 + 2 * NZ),
        out_specs=(VMEM,) * (1 + 2 * NZ),
        scratch_shapes=[
            pltpu.VMEM((NZ * BLK, 2 * BLK), BF),
            pltpu.VMEM((NZ * BLK, 4 * BLK + HALF), BF),
            pltpu.VMEM((2 * BLK, 4 * BLK + HALF), F32),
            pltpu.VMEM((2, NZ, BLK), F32),
        ],
        compiler_params=pltpu.CompilerParams(vmem_limit_bytes=20 * 2**20),
        cost_estimate=pl.CostEstimate(
            flops=5 * 10**9, bytes_accessed=8 * 2**20, transcendentals=0
        ),
        name="group_terms",
    )(place_z, vectors, pair_all, *mixed_all, *hidden_all)
    sums, vectors, term = pl.pallas_call(
        totals_kernel,
        out_shape=(
            jax.ShapeDtypeStruct((2, BLK), F32),
            jax.ShapeDtypeStruct((4, BLK), F32),
            jax.ShapeDtypeStruct((2, BLK), F32),
        ),
        in_specs=[VMEM, VMEM],
        out_specs=(VMEM,) * 3,
        compiler_params=PARAMS,
        name="totals",
    )(exchange(payload, ("x", "c", "y")), vectors)
    grad_shift, grad_gain = sums[0], sums[1]

    scratch = [
        pltpu.VMEM((NZ * BLK, BLK), BF),
        pltpu.VMEM((BLK, NZ * BLK), BF),
        LISTS,
    ]
    cost = pl.CostEstimate(flops=8 * 10**9, bytes_accessed=6 * 2**20, transcendentals=0)
    *send, own_term, grad_m = pl.pallas_call(
        send_kernel,
        out_shape=(
            jax.ShapeDtypeStruct((NX, NY, HALF, BLK), BF),
            jax.ShapeDtypeStruct((NY, NX, HALF, BLK), BF),
            jax.ShapeDtypeStruct((BLK, BLK), F32),
            jax.ShapeDtypeStruct((NZ, BLK, BLK), BF),
        ),
        in_specs=[SMEM] + [VMEM] * (4 + 2 * NZ),
        out_specs=(VMEM,) * 4,
        scratch_shapes=scratch,
        compiler_params=PARAMS,
        cost_estimate=cost,
        name="backward_send",
    )(place_z, vectors, weight_self, weight_neigh, lower, *grads)
    other = [swap(part, "c", 1) for part in send]
    scratch[1] = pltpu.VMEM((HALF, NZ * BLK), BF)
    both = []
    for half in range(2):
        if half:
            grad_m, both = lax.optimization_barrier((grad_m, both))
        keep = pl.pallas_call(
            functools.partial(keep_kernel, half),
            out_shape=(jax.ShapeDtypeStruct((4, HALF, BLK), BF),) * 4,
            in_specs=[SMEM] + [VMEM] * (2 + half),
            out_specs=(VMEM,) * 4,
            scratch_shapes=scratch,
            compiler_params=PARAMS,
            cost_estimate=cost,
            name="backward_keep",
        )(place_z, lower, grad_m, *([other[1]] if half else []))
        if half:
            both.append(list(keep))
        else:
            both.append(
                [(keep[k].astype(F32) + other[0][k].astype(F32)).astype(BF) for k in range(4)]
            )
        if not half:
            both[0], term = lax.optimization_barrier((both[0], term))
            upper = reduce_in(both[0], "x").astype(BF)
            whole = everywhere(term, ("z", "x", "c", "y"), NZ * GROUP)
    whole = [part.reshape(BLK, BLK) for part in jnp.split(whole, 2)]
    both[1], upper = lax.optimization_barrier((both[1], upper))
    upper = reduce_in(upper, "y")
    lower, whole = reduce_in(both[1], "y", whole)
    lower = reduce_in(lower.astype(BF), "x")
    back = jnp.concatenate([upper, lower], axis=0)
    grad_x = (own_term + back).astype(BF)

    return (grad_x, whole[0], whole[1], grad_gain, grad_shift)


def solution(mesh):
    grid = Mesh(mesh.devices.reshape(NX, NC, NY, NZ), ALL)
    row, col = ("x", "c"), ("y", "z")
    placed = (
        P(ALL, None),
        P(),
        P(),
        P(),
        P(),
        P(ALL, None),
        P(row, col, None, None),
        P(row, col, None, None),
        P(row, col, None, None),
        P(row, col, None),
    )
    return jax.shard_map(
        body,
        mesh=grid,
        in_specs=placed,
        out_specs=(P(ALL, None), P(), P(), P(), P()),
        check_vma=False,
    )
```
